32 devices in a mesh: section: 8 (over y, x, core), expert: 4 (over z).
Axes of the slice: x: 2, y: 2, z: 4, core: 2. Of those that a mesh axis runs over, the one named last changes fastest.
Arguments:
- tokens: bfloat16 [16384, 2880], P(('section', 'expert')), may hold values from -6 to 6
- segment_norm_scale: float32 [8, 2880], P('section'), may hold values from 0.1 to 1.9
- expert_choice_table: int32 [4, 16384, 4], P(None, ('section', 'expert')), may hold values from 0 to 127, as said below
- router_weight_table: bfloat16 [4, 16384, 4], P(None, ('section', 'expert')), may hold values from 0.099609375 to 1
- adapter_down_weight: bfloat16 [8, 2880, 128], P('section'), may hold values from -0.109375 to 0.109375
- adapter_up_weight: bfloat16 [8, 128, 2880], P('section'), may hold values from -0.5 to 0.5
- expert_gate_up_weight: bfloat16 [8, 2880, 2, 1440], P('section', None, None, 'expert'), may hold values from -0.109375 to 0.109375
- expert_down_weight: bfloat16 [8, 1440, 2880], P('section', 'expert'), may hold values from -0.15625 to 0.15625
Outputs:
- carried: bfloat16 [16384, 2880], P(('section', 'expert'))
The draws below stay inside these ranges and needn't reach their ends.
Inputs may be any that keep to these rules, and one draw needn't show every extreme that they name: `expert_choice_table`: each row names 4 different experts. Within the rows of one device at one hop, at most 48 rows name expert 0, and in each hop some device has exactly 48 such rows.
All inputs are finite; a program needn't handle non-finite values.
Results may differ from the reference program's by a relative error of at most 0.014.
Values may be sent and summed in bfloat16 or wider, within the bound.
A program may use at most 128 MiB of HBM per device.

```python
import math
import jax
import jax.numpy as jnp
from jax import lax

MODEL_WIDTH = 2880
EXPERTS = 128
HID = 1440
ADAPTER_RANK = 128
TOP = 4
CAP = 48
TOK_DEV = 512
HOPS = 4
TOKENS = 16384
N_SECTION = 8
N_EXPERT = 4


def draw_expert_choice_table(key, part):
    blocks = HOPS * (TOKENS // TOK_DEV)
    key_count, key_full, key_rank, key_base, key_place = jax.random.split(key, 5)
    counts = jax.random.randint(key_count, (blocks,), CAP // 2, CAP + 1)
    full_block = jax.random.randint(key_full, (HOPS,), 0, TOKENS // TOK_DEV)
    block_ids = jnp.arange(blocks, dtype=jnp.int32).reshape(HOPS, TOKENS // TOK_DEV) % (TOKENS // TOK_DEV)
    forced = (block_ids == full_block[:, None]).reshape(-1)
    counts = jnp.where(forced, CAP, counts)
    ranks = jax.vmap(lambda k: jax.random.permutation(k, TOK_DEV))(jax.random.split(key_rank, blocks))
    in_window = ranks < counts[:, None]
    base = jax.random.randint(key_base, (blocks, TOK_DEV, 1), 0, EXPERTS - 1)
    stride = (EXPERTS - 1) // TOP
    others = 1 + (base + stride * jnp.arange(TOP, dtype=jnp.int32)[None, None, :]) % (EXPERTS - 1)
    place = jax.random.randint(key_place, (blocks, TOK_DEV, 1), 0, TOP)
    hit = in_window[..., None] & (jnp.arange(TOP, dtype=jnp.int32)[None, None, :] == place)
    picks = jnp.where(hit, 0, others)
    return picks.reshape(HOPS, TOKENS, TOP).astype(jnp.int32)


def block_levels(key, shape, cuts, least, largest):
    gain = 1.0
    for dim, shards_of in cuts:
        steps = jax.random.uniform(jax.random.fold_in(jax.random.fold_in(key, 6), dim), (shards_of,), jnp.float32, least / len(cuts), largest / len(cuts))
        gain = gain * jnp.repeat(jnp.exp(steps), shape[dim] // shards_of).reshape((-1,) + (1,) * (len(shape) - 1 - dim))
    return gain


def noise(rng, shape, scale, limit, cuts=(), kind=jnp.bfloat16):
    entries = scale * jax.random.normal(rng, shape, jnp.float32)
    if cuts:
        entries = entries * block_levels(rng, shape, cuts, -0.22, 0.18)
    return jnp.clip(entries, -limit, limit).astype(kind)


def setup_inputs(seed: int = 0) -> dict:
    streams_of = jax.random.split(jax.random.key(seed), 9)
    tokens = noise(streams_of[0], (TOKENS, MODEL_WIDTH), 1.0, 6.0, ((0, 32),))
    segment_norm_scale = jnp.clip(1.0 + 0.18 * jax.random.normal(streams_of[1], (N_SECTION, MODEL_WIDTH), jnp.float32), 0.1, 1.9)
    expert_choice_table = draw_expert_choice_table(jax.random.fold_in(streams_of[8], 71), 0)
    router_weight_table = jnp.clip(jnp.exp(math.log(1.0) - 2.306499 * jax.random.uniform(streams_of[3], (HOPS, TOKENS, TOP), jnp.float32) ** block_levels(streams_of[3], (HOPS, TOKENS, TOP), ((1, 32),), -0.2, 0.2)), 0.099609375, 1.0).astype(jnp.bfloat16)
    adapter_down_weight = noise(streams_of[4], (N_SECTION, MODEL_WIDTH, ADAPTER_RANK), MODEL_WIDTH ** -0.5, 0.109375, ((0, 8),))
    adapter_up_weight = noise(streams_of[5], (N_SECTION, ADAPTER_RANK, MODEL_WIDTH), ADAPTER_RANK ** -0.5, 0.5, ((0, 8),))
    expert_gate_up_weight = noise(streams_of[6], (N_SECTION, MODEL_WIDTH, 2, HID), MODEL_WIDTH ** -0.5, 0.109375, ((0, 8), (3, 4)))
    expert_down_weight = noise(streams_of[7], (N_SECTION, HID, MODEL_WIDTH), HID ** -0.5, 0.15625, ((0, 8), (1, 4)))
    return {"tokens": tokens, "segment_norm_scale": segment_norm_scale, "expert_choice_table": expert_choice_table, "router_weight_table": router_weight_table, "adapter_down_weight": adapter_down_weight, "adapter_up_weight": adapter_up_weight, "expert_gate_up_weight": expert_gate_up_weight, "expert_down_weight": expert_down_weight}


def window_tables(expert_choice_rows, mix_row):
    flags = jnp.any(expert_choice_rows == 0, axis=-1)
    flag_int = flags.astype(jnp.int32)
    position = jnp.cumsum(flag_int) - flag_int
    slot_index = jnp.where(flags, position, CAP).astype(jnp.int32)
    select = (jnp.arange(CAP, dtype=jnp.int32)[:, None] == slot_index[None, :]).astype(jnp.bfloat16)
    mix_values = mix_row.astype(jnp.float32)
    chosen = lax.optimization_barrier(jnp.sum(jnp.where(expert_choice_rows == 0, mix_values, 0.0), axis=-1))
    share = chosen / lax.optimization_barrier(jnp.sum(mix_values, axis=-1))
    return (select, share)

def relay_segment_advance(packed):
    travelling_state, expert_choice_rows, router_weight_rows, gain_row, adapter_down_factor, adapter_up_factor, weight_in, weight_out = packed
    values = travelling_state.astype(jnp.float32)
    scale = lax.rsqrt(lax.optimization_barrier(jnp.mean(values * values, axis=-1, keepdims=True)) + 1e-05)
    normed = (values * scale * gain_row.astype(jnp.float32)).astype(jnp.bfloat16)
    flat_normed = normed.reshape(N_EXPERT * TOK_DEV, MODEL_WIDTH)
    low = jnp.dot(flat_normed, adapter_down_factor, preferred_element_type=jnp.float32).astype(jnp.bfloat16)
    adapter = jnp.dot(low, adapter_up_factor, preferred_element_type=jnp.float32).reshape(N_EXPERT, TOK_DEV, MODEL_WIDTH)
    adapted = (values + adapter).astype(jnp.bfloat16)
    select, share = jax.vmap(window_tables)(expert_choice_rows, router_weight_rows)
    slot_rows = jax.vmap(lambda s, n: jnp.dot(s, n, preferred_element_type=jnp.float32))(select, normed).astype(jnp.bfloat16)
    rows = slot_rows.reshape(N_EXPERT * CAP, MODEL_WIDTH)
    joined = jnp.dot(rows, weight_in.reshape(MODEL_WIDTH, 2 * HID), preferred_element_type=jnp.float32)
    gate_part = joined[:, :HID]
    up_part = joined[:, HID:]
    activated = (gate_part * jax.nn.sigmoid(1.702 * gate_part) * (up_part + 1.0)).astype(jnp.bfloat16)
    hid_dev = HID // N_EXPERT
    expert_out = jnp.zeros((N_EXPERT * CAP, MODEL_WIDTH), jnp.float32)
    for block in range(N_EXPERT):
        part_value = jnp.dot(activated[:, block * hid_dev:(block + 1) * hid_dev], weight_out[block * hid_dev:(block + 1) * hid_dev], preferred_element_type=jnp.float32).astype(jnp.bfloat16)
        part_value = lax.optimization_barrier(part_value)
        expert_out = expert_out + part_value.astype(jnp.float32)
    expert_out = expert_out.reshape(N_EXPERT, CAP, MODEL_WIDTH)
    picked = jax.vmap(lambda s, e: jnp.dot(s.astype(jnp.float32).T, e, precision=lax.Precision.HIGHEST))(select, expert_out)
    return (adapted.astype(jnp.float32) + share[..., None] * picked).astype(jnp.bfloat16)

def reference(tokens, segment_norm_scale, expert_choice_table, router_weight_table, adapter_down_weight, adapter_up_weight, expert_gate_up_weight, expert_down_weight):
    travelling_state = tokens.reshape(N_SECTION, N_EXPERT, TOK_DEV, MODEL_WIDTH)
    for hop_index in range(HOPS):
        expert_choice_rows = expert_choice_table[hop_index].reshape(N_SECTION, N_EXPERT, TOK_DEV, TOP)
        router_weight_rows = router_weight_table[hop_index].reshape(N_SECTION, N_EXPERT, TOK_DEV, TOP)
        travelling_state = lax.map(relay_segment_advance, (travelling_state, expert_choice_rows, router_weight_rows, segment_norm_scale, adapter_down_weight, adapter_up_weight, expert_gate_up_weight, expert_down_weight))
        travelling_state = jnp.roll(travelling_state, 1, axis=0)
    return travelling_state.reshape(TOKENS, MODEL_WIDTH)
```

```python
import functools

import jax
import jax.numpy as jnp
from jax import lax
from jax.experimental import pallas as pl
from jax.experimental.pallas import tpu as pltpu
from jax.sharding import PartitionSpec as P

CAP = 48
LEFT, RIGHT = 0, 1


def row_tile(width):
    for tile in (320, 192, 64, 16):
        if width % tile == 0:
            return tile
    return width


def relay_kernel(
    n_section,
    n_expert,
    tokens_ref,
    gain_ref,
    choice_ref,
    router_ref,
    down_ref,
    up_ref,
    weight_in_ref,
    weight_out_ref,
    x_ref,
    normed,
    adapted,
    arrived,
    gain_col,
    square_sum,
    own_rows,
    gathered,
    partials,
    returned,
    expert_sum,
    expert_own,
    expert_in,
    meta_own,
    meta_in,
    down_v,
    up_v,
    weight_in_v,
    weight_out_v,
    load_sem,
    ag_send,
    ag_recv,
    rs_send,
    rs_recv,
    x_send,
    x_recv,
    e_send,
    e_recv,
    m_send,
    m_recv,
):
    section = lax.axis_index("section")
    expert = lax.axis_index("expert")
    hops = choice_ref.shape[0]
    width, rows = x_ref.shape
    tile = row_tile(width)
    steps = n_expert - 1
    following = lax.rem(section + 1, n_section)
    previous = lax.rem(section + n_section - 1, n_section)

    def place(to_section, to_expert):
        return {"section": to_section, "expert": to_expert}

    loads = [
        pltpu.make_async_copy(source, target, load_sem.at[i])
        for i, (source, target) in enumerate(
            (
                (tokens_ref, x_ref),
                (down_ref, down_v),
                (up_ref, up_v),
                (weight_in_ref, weight_in_v),
                (weight_out_ref, weight_out_v),
            )
        )
    ]
    for load in loads:
        load.start()

    barrier = pltpu.get_barrier_semaphore()
    for target in (
        place(following, expert),
        place(previous, expert),
        place(section, lax.rem(expert + 1, n_expert)),
        place(section, lax.rem(expert + n_expert - 1, n_expert)),
        place(section, lax.rem(expert + 2, n_expert)),
    ):
        pl.semaphore_signal(barrier, inc=1, device_id=target, device_id_type=pl.DeviceIdType.MESH)

    before = (
        lax.broadcasted_iota(jnp.int32, (rows, rows), 0)
        < lax.broadcasted_iota(jnp.int32, (rows, rows), 1)
    ).astype(jnp.float32).astype(jnp.bfloat16)
    meta_own[...] = jnp.zeros_like(meta_own)
    for hop in range(hops):
        picks = choice_ref[hop]
        mix = router_ref[hop].astype(jnp.float32)
        here = (picks == 0).astype(jnp.float32)
        flag = jnp.max(here, axis=0, keepdims=True)
        position = jnp.dot(
            jnp.broadcast_to(flag, (16, rows)).astype(jnp.bfloat16),
            before,
            preferred_element_type=jnp.float32,
        )[:1]
        chosen = jnp.sum(here * mix, axis=0, keepdims=True)
        total = jnp.sum(mix, axis=0, keepdims=True)
        meta_own[hop, 0:1, :] = jnp.where(flag > 0.0, position, float(CAP))
        meta_own[hop, 1:2, :] = chosen / total

    for start in range(0, width, 128):
        stop = min(start + 128, width)
        piece = jnp.broadcast_to(gain_ref[0:1, start:stop], (128, stop - start))
        gain_col[start:stop, :] = piece.T

    pl.semaphore_wait(barrier, 5)

    def remote(source, target, send, recv, device):
        return pltpu.make_async_remote_copy(
            src_ref=source,
            dst_ref=target,
            send_sem=send,
            recv_sem=recv,
            device_id=device,
            device_id_type=pl.DeviceIdType.MESH,
        )

    meta_copy = remote(meta_own, meta_in, m_send, m_recv, place(following, expert))
    meta_copy.start()

    def tiles(body):
        def step(i, carry):
            body(pl.ds(pl.multiple_of(i * tile, tile), tile))
            return carry

        lax.fori_loop(0, width // tile, step, 0)

    def add_squares(values):
        square_sum[...] += jnp.sum((values * values).reshape(tile // 8, 8, rows), axis=0)

    loads[0].wait()
    square_sum[...] = jnp.zeros_like(square_sum)

    def first_squares(at):
        add_squares(x_ref[at, :].astype(jnp.float32))

    tiles(first_squares)

    def one_hot(meta, hop):
        slots = lax.broadcasted_iota(jnp.int32, (CAP, rows), 0).astype(jnp.float32)
        return jnp.where(slots == meta[hop, 0:1, :], 1.0, 0.0).astype(jnp.bfloat16)

    def expert_partial(block):
        gate = lax.dot_general(
            block, weight_in_v[0], (((1,), (1,)), ((), ())), preferred_element_type=jnp.float32
        )
        up = lax.dot_general(
            block, weight_in_v[1], (((1,), (1,)), ((), ())), preferred_element_type=jnp.float32
        )
        activated = (gate * jax.nn.sigmoid(1.702 * gate) * (up + 1.0)).astype(jnp.bfloat16)
        return jnp.dot(
            activated, weight_out_v[...], preferred_element_type=jnp.float32
        ).astype(jnp.bfloat16)

    def left_at(distance):
        return expert >= distance

    def right_at(distance):
        return expert + distance < n_expert

    def gather_send(hop, k, side):
        source = own_rows.at[hop] if k == 0 else gathered.at[hop, k - 1, side]
        step = 1 if side == LEFT else -1
        return remote(
            source,
            gathered.at[hop, k, side],
            ag_send.at[hop, k, side],
            ag_recv.at[hop, k, side],
            place(section, lax.rem(expert + step + n_expert, n_expert)),
        )

    def gather_sends(hop, k):
        return (
            (left_at(k) & right_at(1), gather_send(hop, k, LEFT)),
            (right_at(k) & left_at(1), gather_send(hop, k, RIGHT)),
        )

    def partial_send(hop, k, side):
        away = -(k + 1) if side == LEFT else k + 1
        return remote(
            partials.at[k, side],
            returned.at[hop, k, 1 - side],
            rs_send.at[hop, k, side],
            rs_recv.at[hop, k, 1 - side],
            place(section, lax.rem(expert + away + n_expert, n_expert)),
        )

    def on_side(side, distance):
        return left_at(distance) if side == LEFT else right_at(distance)

    def hop_body(hop, carry):
        scale = lax.rsqrt(
            jnp.sum(square_sum[...], axis=0, keepdims=True) * (1.0 / width) + 1e-05
        )

        def normalise(at):
            gain = jnp.concatenate([gain_col[at, :]] * (rows // 128), axis=1)
            normed[at, :] = (x_ref[at, :].astype(jnp.float32) * scale * gain).astype(jnp.bfloat16)

        tiles(normalise)
        own_rows[hop] = lax.dot_general(
            one_hot(meta_own, hop),
            normed[...],
            (((1,), (1,)), ((), ())),
            preferred_element_type=jnp.float32,
        ).astype(jnp.bfloat16)
        for valid, copy in gather_sends(hop, 0):
            pl.when(valid)(copy.start)

        @pl.when(hop == 0)
        def _():
            loads[1].wait()
            loads[2].wait()

        low = lax.dot_general(
            down_v[...], normed[...], (((0,), (0,)), ((), ())), preferred_element_type=jnp.float32
        ).astype(jnp.bfloat16)

        def adapt(at):
            adapted[at, :] = (
                x_ref[at, :].astype(jnp.float32)
                + jnp.dot(up_v[at, :], low, preferred_element_type=jnp.float32)
            ).astype(jnp.bfloat16)

        tiles(adapt)
        stream_copy = remote(
            adapted, arrived.at[hop], x_send.at[hop], x_recv.at[hop], place(following, expert)
        )
        stream_copy.start()

        def take_and_forward(k):
            for side in (LEFT, RIGHT):
                pl.when(on_side(side, k + 1))(gather_send(hop, k, side).wait_recv)
            if k + 1 < steps:
                for valid, copy in gather_sends(hop, k + 1):
                    pl.when(valid)(copy.start)

        take_and_forward(0)

        @pl.when(hop == 0)
        def _():
            loads[3].wait()
            loads[4].wait()

        expert_sum[...] = expert_partial(own_rows[hop]).astype(jnp.float32)
        for k in range(steps):

            @pl.when(left_at(k + 1) | right_at(k + 1))
            def _(k=k):
                block = gathered[hop, k].reshape(2 * CAP, width)
                partials[k] = expert_partial(block).reshape(2, CAP, width)

            for side in (LEFT, RIGHT):
                pl.when(on_side(side, k + 1))(partial_send(hop, k, side).start)
            if k + 1 < steps:
                take_and_forward(k + 1)

        for k in range(steps):
            for side in (LEFT, RIGHT):

                @pl.when(on_side(side, k + 1))
                def _(k=k, side=side):
                    partial_send(hop, k, 1 - side).wait_recv()
                    expert_sum[...] += returned[hop, k, side].astype(jnp.float32)

        expert_own[hop] = expert_sum[...].astype(jnp.bfloat16)
        expert_copy = remote(
            expert_own.at[hop],
            expert_in.at[hop],
            e_send.at[hop],
            e_recv.at[hop],
            place(following, expert),
        )
        expert_copy.start()

        for k in range(steps):
            for valid, copy in gather_sends(hop, k):
                pl.when(valid)(copy.wait_send)
            for side in (LEFT, RIGHT):
                pl.when(on_side(side, k + 1))(partial_send(hop, k, side).wait_send)

        @pl.when(hop == 0)
        def _():
            meta_copy.wait()

        stream_copy.wait()
        expert_copy.wait()
        spread = one_hot(meta_in, hop)
        share = meta_in[hop, 1:2, :]
        square_sum[...] = jnp.zeros_like(square_sum)
        lanes = 384
        for start in range(0, width, lanes):
            stop = min(start + lanes, width)
            picked = lax.dot_general(
                expert_in[hop, :, start:stop],
                spread,
                (((0,), (0,)), ((), ())),
                preferred_element_type=jnp.float32,
            )
            moved = (
                arrived[hop, start:stop, :].astype(jnp.float32) + share * picked
            ).astype(jnp.bfloat16)
            x_ref[start:stop, :] = moved
            values = moved.astype(jnp.float32)
            square_sum[...] += jnp.sum(
                (values * values).reshape((stop - start) // 8, 8, rows), axis=0
            )
        return carry

    lax.fori_loop(0, hops, hop_body, 0)


def body(
    n_section,
    n_expert,
    tokens,
    segment_norm_scale,
    expert_choice_table,
    router_weight_table,
    adapter_down_weight,
    adapter_up_weight,
    expert_gate_up_weight,
    expert_down_weight,
):
    rows, width = tokens.shape
    hops, _, top = expert_choice_table.shape
    rank = adapter_down_weight.shape[2]
    hid = expert_down_weight.shape[1]
    steps = n_expert - 1
    half = jnp.bfloat16
    full = jnp.float32
    block = (CAP, width)
    dma = pltpu.SemaphoreType.DMA
    flops = hops * (4 * rows * width * rank + 6 * n_expert * CAP * width * hid)
    out = pl.pallas_call(
        functools.partial(relay_kernel, n_section, n_expert),
        out_shape=jax.ShapeDtypeStruct((width, rows), half),
        in_specs=[
            pl.BlockSpec(memory_space=pl.ANY),
            pl.BlockSpec(memory_space=pltpu.VMEM),
            pl.BlockSpec(memory_space=pltpu.VMEM),
            pl.BlockSpec(memory_space=pltpu.VMEM),
            pl.BlockSpec(memory_space=pl.ANY),
            pl.BlockSpec(memory_space=pl.ANY),
            pl.BlockSpec(memory_space=pl.ANY),
            pl.BlockSpec(memory_space=pl.ANY),
        ],
        out_specs=pl.BlockSpec(memory_space=pltpu.VMEM),
        scratch_shapes=[
            pltpu.VMEM((width, rows), half),
            pltpu.VMEM((width, rows), half),
            pltpu.VMEM((hops, width, rows), half),
            pltpu.VMEM((width, 128), full),
            pltpu.VMEM((8, rows), full),
            pltpu.VMEM((hops,) + block, half),
            pltpu.VMEM((hops, steps, 2) + block, half),
            pltpu.VMEM((steps, 2) + block, half),
            pltpu.VMEM((hops, steps, 2) + block, half),
            pltpu.VMEM(block, full),
            pltpu.VMEM((hops,) + block, half),
            pltpu.VMEM((hops,) + block, half),
            pltpu.VMEM((hops, 8, rows), full),
            pltpu.VMEM((hops, 8, rows), full),
            pltpu.VMEM((width, rank), half),
            pltpu.VMEM((width, rank), half),
            pltpu.VMEM((2, hid, width), half),
            pltpu.VMEM((hid, width), half),
            dma((5,)),
            dma((hops, steps, 2)),
            dma((hops, steps, 2)),
            dma((hops, steps, 2)),
            dma((hops, steps, 2)),
            dma((hops,)),
            dma((hops,)),
            dma((hops,)),
            dma((hops,)),
            dma,
            dma,
        ],
        compiler_params=pltpu.CompilerParams(
            collective_id=0, has_side_effects=True, vmem_limit_bytes=60 * 2**20
        ),
        cost_estimate=pl.CostEstimate(
            flops=flops, bytes_accessed=16 * 2**20, transcendentals=hops * n_expert * CAP * hid
        ),
    )(
        tokens.T,
        segment_norm_scale,
        jnp.transpose(expert_choice_table, (0, 2, 1)),
        jnp.transpose(router_weight_table, (0, 2, 1)),
        adapter_down_weight[0],
        adapter_up_weight[0].T,
        jnp.transpose(expert_gate_up_weight[0], (1, 2, 0)),
        expert_down_weight[0],
    )
    return out.T


def solution(mesh):
    return jax.shard_map(
        functools.partial(body, mesh.shape["section"], mesh.shape["expert"]),
        mesh=mesh,
        in_specs=(
            P(("section", "expert"), None),
            P("section", None),
            P(None, ("section", "expert"), None),
            P(None, ("section", "expert"), None),
            P("section", None, None),
            P("section", None, None),
            P("section", None, None, "expert"),
            P("section", "expert", None),
        ),
        out_specs=P(("section", "expert"), None),
        check_vma=False,
    )
```

```python
import functools

import jax
import jax.numpy as jnp
from jax import lax
from jax.experimental import pallas as pl
from jax.experimental.pallas import tpu as pltpu
from jax.sharding import PartitionSpec as P

CAP = 48
LEFT, RIGHT = 0, 1


def row_tile(width):
    for tile in (320, 192, 64, 16):
        if width % tile == 0:
            return tile
    return width


def relay_kernel(
    n_section,
    n_expert,
    tokens_ref,
    gain_ref,
    choice_ref,
    router_ref,
    down_ref,
    up_ref,
    weight_in_ref,
    weight_out_ref,
    x_ref,
    normed,
    arrived,
    gain_col,
    square_sum,
    own_rows,
    gathered,
    partials,
    returned,
    expert_sum,
    expert_own,
    expert_in,
    raw_rows,
    low_own,
    low_in,
    up_previous,
    meta_own,
    meta_in,
    down_v,
    up_v,
    weight_in_v,
    weight_out_v,
    load_sem,
    ag_send,
    ag_recv,
    rs_send,
    rs_recv,
    x_send,
    x_recv,
    e_send,
    e_recv,
    m_send,
    m_recv,
    l_send,
    l_recv,
    u_send,
    u_recv,
):
    section = lax.axis_index("section")
    expert = lax.axis_index("expert")
    hops = choice_ref.shape[0]
    width, rows = x_ref.shape
    tile = row_tile(width)
    steps = n_expert - 1
    following = lax.rem(section + 1, n_section)
    previous = lax.rem(section + n_section - 1, n_section)

    def place(to_section, to_expert):
        return {"section": to_section, "expert": to_expert}

    loads = [
        pltpu.make_async_copy(source, target, load_sem.at[i])
        for i, (source, target) in enumerate(
            (
                (tokens_ref, x_ref),
                (down_ref, down_v),
                (up_ref, up_v),
                (weight_in_ref, weight_in_v),
                (weight_out_ref, weight_out_v),
            )
        )
    ]
    for load in loads:
        load.start()

    barrier = pltpu.get_barrier_semaphore()
    for target in (
        place(following, expert),
        place(previous, expert),
        place(section, lax.rem(expert + 1, n_expert)),
        place(section, lax.rem(expert + n_expert - 1, n_expert)),
        place(section, lax.rem(expert + 2, n_expert)),
    ):
        pl.semaphore_signal(barrier, inc=1, device_id=target, device_id_type=pl.DeviceIdType.MESH)

    before = (
        lax.broadcasted_iota(jnp.int32, (rows, rows), 0)
        < lax.broadcasted_iota(jnp.int32, (rows, rows), 1)
    ).astype(jnp.float32).astype(jnp.bfloat16)
    meta_own[...] = jnp.zeros_like(meta_own)
    for hop in range(hops):
        picks = choice_ref[hop]
        mix = router_ref[hop].astype(jnp.float32)
        here = (picks == 0).astype(jnp.float32)
        flag = jnp.max(here, axis=0, keepdims=True)
        position = jnp.dot(
            jnp.broadcast_to(flag, (16, rows)).astype(jnp.bfloat16),
            before,
            preferred_element_type=jnp.float32,
        )[:1]
        chosen = jnp.sum(here * mix, axis=0, keepdims=True)
        total = jnp.sum(mix, axis=0, keepdims=True)
        meta_own[hop, 0:1, :] = jnp.where(flag > 0.0, position, float(CAP))
        meta_own[hop, 1:2, :] = chosen / total

    for start in range(0, width, 128):
        stop = min(start + 128, width)
        piece = jnp.broadcast_to(gain_ref[0:1, start:stop], (128, stop - start))
        gain_col[start:stop, :] = piece.T

    pl.semaphore_wait(barrier, 5)

    def remote(source, target, send, recv, device):
        return pltpu.make_async_remote_copy(
            src_ref=source,
            dst_ref=target,
            send_sem=send,
            recv_sem=recv,
            device_id=device,
            device_id_type=pl.DeviceIdType.MESH,
        )

    def tiles(body):
        def step(i, carry):
            body(pl.ds(pl.multiple_of(i * tile, tile), tile))
            return carry

        lax.fori_loop(0, width // tile, step, 0)

    pieces = [(start, min(start + 768, width)) for start in range(0, width, 768)]

    def lane_tiles(start, stop):
        return [(at, min(at + 384, stop)) for at in range(start, stop, 384)]

    def stream_copy(hop, c):
        start, stop = pieces[c]
        return remote(
            x_ref.at[start:stop],
            arrived.at[hop, start:stop],
            x_send.at[hop, c],
            x_recv.at[hop, c],
            place(following, expert),
        )

    loads[0].wait()
    for c in range(len(pieces)):
        stream_copy(0, c).start()
    meta_copy = remote(meta_own, meta_in, m_send, m_recv, place(following, expert))
    meta_copy.start()
    loads[2].wait()
    up_copy = remote(up_v, up_previous, u_send, u_recv, place(following, expert))
    up_copy.start()

    def one_hot(meta, hop):
        slots = lax.broadcasted_iota(jnp.int32, (CAP, rows), 0).astype(jnp.float32)
        return jnp.where(slots == meta[hop, 0:1, :], 1.0, 0.0).astype(jnp.bfloat16)

    def select_rows(select, values):
        return lax.dot_general(
            select, values, (((1,), (1,)), ((), ())), preferred_element_type=jnp.float32
        )

    raw_rows[...] = select_rows(one_hot(meta_own, 0), x_ref[...])

    def settle(hop, send_on):
        spread = one_hot(meta_in, hop)
        share = meta_in[hop, 1:2, :]
        square_sum[...] = jnp.zeros_like(square_sum)
        for c, (first, last) in enumerate(pieces):
            stream_copy(hop, c).wait_send()
            for start, stop in lane_tiles(first, last):
                picked = lax.dot_general(
                    expert_in[hop, :, start:stop],
                    spread,
                    (((0,), (0,)), ((), ())),
                    preferred_element_type=jnp.float32,
                )
                moved = (
                    arrived[hop, start:stop, :].astype(jnp.float32) + share * picked
                ).astype(jnp.bfloat16)
                x_ref[start:stop, :] = moved
                if send_on:
                    values = moved.astype(jnp.float32)
                    square_sum[...] += jnp.sum(
                        (values * values).reshape((stop - start) // 8, 8, rows), axis=0
                    )
            if send_on:
                stream_copy(hop + 1, c).start()

    def expert_partial(block):
        gate = lax.dot_general(
            block, weight_in_v[0], (((1,), (1,)), ((), ())), preferred_element_type=jnp.float32
        )
        up = lax.dot_general(
            block, weight_in_v[1], (((1,), (1,)), ((), ())), preferred_element_type=jnp.float32
        )
        activated = (gate * jax.nn.sigmoid(1.702 * gate) * (up + 1.0)).astype(jnp.bfloat16)
        return jnp.dot(
            activated, weight_out_v[...], preferred_element_type=jnp.float32
        ).astype(jnp.bfloat16)

    def left_at(distance):
        return expert >= distance

    def right_at(distance):
        return expert + distance < n_expert

    def gather_send(hop, k, side):
        source = own_rows.at[hop] if k == 0 else gathered.at[hop, k - 1, side]
        step = 1 if side == LEFT else -1
        return remote(
            source,
            gathered.at[hop, k, side],
            ag_send.at[hop, k, side],
            ag_recv.at[hop, k, side],
            place(section, lax.rem(expert + step + n_expert, n_expert)),
        )

    def gather_sends(hop, k):
        return (
            (left_at(k) & right_at(1), gather_send(hop, k, LEFT)),
            (right_at(k) & left_at(1), gather_send(hop, k, RIGHT)),
        )

    def partial_send(hop, k, side):
        away = -(k + 1) if side == LEFT else k + 1
        return remote(
            partials.at[k, side],
            returned.at[hop, k, 1 - side],
            rs_send.at[hop, k, side],
            rs_recv.at[hop, k, 1 - side],
            place(section, lax.rem(expert + away + n_expert, n_expert)),
        )

    def on_side(side, distance):
        return left_at(distance) if side == LEFT else right_at(distance)

    def hop_body(hop, carry):
        raw = raw_rows[...]
        row_scale = lax.rsqrt(
            jnp.sum(raw * raw, axis=1, keepdims=True) * (1.0 / width) + 1e-05
        )
        own_rows[hop] = (raw * row_scale * gain_ref[...]).astype(jnp.bfloat16)
        for valid, copy in gather_sends(hop, 0):
            pl.when(valid)(copy.start)

        @pl.when(hop == 0)
        def _():
            square_sum[...] = jnp.zeros_like(square_sum)

            def first_squares(at):
                values = x_ref[at, :].astype(jnp.float32)
                square_sum[...] += jnp.sum(
                    (values * values).reshape(tile // 8, 8, rows), axis=0
                )

            tiles(first_squares)
            loads[1].wait()

        @pl.when(hop > 0)
        def _():
            settle(hop - 1, True)

        scale = lax.rsqrt(
            jnp.sum(square_sum[...], axis=0, keepdims=True) * (1.0 / width) + 1e-05
        )

        def normalise(at):
            gain = jnp.concatenate([gain_col[at, :]] * (rows // 128), axis=1)
            normed[at, :] = (x_ref[at, :].astype(jnp.float32) * scale * gain).astype(jnp.bfloat16)

        tiles(normalise)
        low_own[hop] = lax.dot_general(
            down_v[...], normed[...], (((0,), (0,)), ((), ())), preferred_element_type=jnp.float32
        ).astype(jnp.bfloat16)
        low_copy = remote(
            low_own.at[hop], low_in.at[hop], l_send.at[hop], l_recv.at[hop], place(following, expert)
        )
        low_copy.start()

        def take_and_forward(k):
            for side in (LEFT, RIGHT):
                pl.when(on_side(side, k + 1))(gather_send(hop, k, side).wait_recv)
            if k + 1 < steps:
                for valid, copy in gather_sends(hop, k + 1):
                    pl.when(valid)(copy.start)

        take_and_forward(0)

        @pl.when(hop == 0)
        def _():
            loads[3].wait()
            loads[4].wait()

        expert_sum[...] = expert_partial(own_rows[hop]).astype(jnp.float32)
        for k in range(steps):

            @pl.when(left_at(k + 1) | right_at(k + 1))
            def _(k=k):
                block = gathered[hop, k].reshape(2 * CAP, width)
                partials[k] = expert_partial(block).reshape(2, CAP, width)

            for side in (LEFT, RIGHT):
                pl.when(on_side(side, k + 1))(partial_send(hop, k, side).start)
            if k + 1 < steps:
                take_and_forward(k + 1)

        @pl.when(hop == 0)
        def _():
            meta_copy.wait()
            up_copy.wait()

        low_copy.wait()
        more = hop + 1 < hops

        def adapt(c):
            first, last = pieces[c]
            stream_copy(hop, c).wait_recv()
            for start, stop in lane_tiles(first, last):
                arrived[hop, start:stop, :] = (
                    arrived[hop, start:stop, :].astype(jnp.float32)
                    + jnp.dot(
                        up_previous[start:stop, :], low_in[hop], preferred_element_type=jnp.float32
                    )
                ).astype(jnp.bfloat16)

            @pl.when(more)
            def _():
                raw_rows[:, first:last] = select_rows(
                    one_hot(meta_own, hop + 1), arrived[hop, first:last, :]
                )

        for c in range(len(pieces) - 1):
            adapt(c)

        for k in range(steps):
            for side in (LEFT, RIGHT):

                @pl.when(on_side(side, k + 1))
                def _(k=k, side=side):
                    partial_send(hop, k, 1 - side).wait_recv()
                    expert_sum[...] += returned[hop, k, side].astype(jnp.float32)

        expert_own[hop] = expert_sum[...].astype(jnp.bfloat16)
        expert_copy = remote(
            expert_own.at[hop],
            expert_in.at[hop],
            e_send.at[hop],
            e_recv.at[hop],
            place(following, expert),
        )
        expert_copy.start()
        adapt(len(pieces) - 1)

        for k in range(steps):
            for valid, copy in gather_sends(hop, k):
                pl.when(valid)(copy.wait_send)
            for side in (LEFT, RIGHT):
                pl.when(on_side(side, k + 1))(partial_send(hop, k, side).wait_send)

        @pl.when(more)
        def _():
            chosen = one_hot(meta_own, hop + 1)
            meeting = select_rows(chosen, one_hot(meta_in, hop)).astype(jnp.bfloat16)
            share = jnp.sum(
                chosen.astype(jnp.float32) * meta_in[hop, 1:2, :], axis=1, keepdims=True
            )
            expert_copy.wait()
            picked = jnp.dot(meeting, expert_in[hop], preferred_element_type=jnp.float32)
            raw_rows[...] = (
                (raw_rows[...] + share * picked).astype(jnp.bfloat16).astype(jnp.float32)
            )

        @pl.when(hop + 1 == hops)
        def _():
            expert_copy.wait()

        return carry

    lax.fori_loop(0, hops, hop_body, 0)
    settle(hops - 1, False)


def body(
    n_section,
    n_expert,
    tokens,
    segment_norm_scale,
    expert_choice_table,
    router_weight_table,
    adapter_down_weight,
    adapter_up_weight,
    expert_gate_up_weight,
    expert_down_weight,
):
    rows, width = tokens.shape
    hops, _, top = expert_choice_table.shape
    rank = adapter_down_weight.shape[2]
    hid = expert_down_weight.shape[1]
    steps = n_expert - 1
    stream_pieces = pl.cdiv(width, 768)
    half = jnp.bfloat16
    full = jnp.float32
    block = (CAP, width)
    dma = pltpu.SemaphoreType.DMA
    flops = hops * (4 * rows * width * rank + 6 * n_expert * CAP * width * hid)
    out = pl.pallas_call(
        functools.partial(relay_kernel, n_section, n_expert),
        out_shape=jax.ShapeDtypeStruct((width, rows), half),
        in_specs=[
            pl.BlockSpec(memory_space=pl.ANY),
            pl.BlockSpec(memory_space=pltpu.VMEM),
            pl.BlockSpec(memory_space=pltpu.VMEM),
            pl.BlockSpec(memory_space=pltpu.VMEM),
            pl.BlockSpec(memory_space=pl.ANY),
            pl.BlockSpec(memory_space=pl.ANY),
            pl.BlockSpec(memory_space=pl.ANY),
            pl.BlockSpec(memory_space=pl.ANY),
        ],
        out_specs=pl.BlockSpec(memory_space=pltpu.VMEM),
        scratch_shapes=[
            pltpu.VMEM((width, rows), half),
            pltpu.VMEM((hops, width, rows), half),
            pltpu.VMEM((width, 128), full),
            pltpu.VMEM((8, rows), full),
            pltpu.VMEM((hops,) + block, half),
            pltpu.VMEM((hops, steps, 2) + block, half),
            pltpu.VMEM((steps, 2) + block, half),
            pltpu.VMEM((hops, steps, 2) + block, half),
            pltpu.VMEM(block, full),
            pltpu.VMEM((hops,) + block, half),
            pltpu.VMEM((hops,) + block, half),
            pltpu.VMEM(block, full),
            pltpu.VMEM((hops, rank, rows), half),
            pltpu.VMEM((hops, rank, rows), half),
            pltpu.VMEM((width, rank), half),
            pltpu.VMEM((hops, 8, rows), full),
            pltpu.VMEM((hops, 8, rows), full),
            pltpu.VMEM((width, rank), half),
            pltpu.VMEM((width, rank), half),
            pltpu.VMEM((2, hid, width), half),
            pltpu.VMEM((hid, width), half),
            dma((5,)),
            dma((hops, steps, 2)),
            dma((hops, steps, 2)),
            dma((hops, steps, 2)),
            dma((hops, steps, 2)),
            dma((hops, stream_pieces)),
            dma((hops, stream_pieces)),
            dma((hops,)),
            dma((hops,)),
            dma,
            dma,
            dma((hops,)),
            dma((hops,)),
            dma,
            dma,
        ],
        compiler_params=pltpu.CompilerParams(
            collective_id=0, has_side_effects=True, vmem_limit_bytes=60 * 2**20
        ),
        cost_estimate=pl.CostEstimate(
            flops=flops, bytes_accessed=16 * 2**20, transcendentals=hops * n_expert * CAP * hid
        ),
    )(
        tokens.T,
        segment_norm_scale,
        jnp.transpose(expert_choice_table, (0, 2, 1)),
        jnp.transpose(router_weight_table, (0, 2, 1)),
        adapter_down_weight[0],
        adapter_up_weight[0].T,
        jnp.transpose(expert_gate_up_weight[0], (1, 2, 0)),
        expert_down_weight[0],
    )
    return out.T


def solution(mesh):
    return jax.shard_map(
        functools.partial(body, mesh.shape["section"], mesh.shape["expert"]),
        mesh=mesh,
        in_specs=(
            P(("section", "expert"), None),
            P("section", None),
            P(None, ("section", "expert"), None),
            P(None, ("section", "expert"), None),
            P("section", None, None),
            P("section", None, None),
            P("section", None, None, "expert"),
            P("section", "expert", None),
        ),
        out_specs=P(("section", "expert"), None),
        check_vma=False,
    )
```

```python
import functools

import jax
import jax.numpy as jnp
from jax import lax
from jax.experimental import pallas as pl
from jax.experimental.pallas import tpu as pltpu
from jax.sharding import PartitionSpec as P

CAP = 48
ROWS = 16
LEFT, RIGHT = 0, 1


def row_tile(width):
    for tile in (320, 192, 64, 16):
        if width % tile == 0:
            return tile
    return width


def relay_kernel(
    n_section,
    n_expert,
    tokens_ref,
    gain_ref,
    choice_ref,
    router_ref,
    down_ref,
    up_ref,
    weight_in_ref,
    weight_out_ref,
    x_ref,
    normed,
    arrived,
    gain_col,
    square_sum,
    own_rows,
    gathered,
    partials,
    returned,
    relayed,
    expert_sum,
    expert_own,
    expert_in,
    raw_rows,
    low_own,
    low_in,
    up_previous,
    meta_own,
    meta_in,
    down_v,
    up_v,
    weight_in_v,
    weight_out_v,
    load_sem,
    ag_send,
    ag_recv,
    rs_send,
    rs_recv,
    relay_recv,
    x_send,
    x_recv,
    e_send,
    e_recv,
    m_send,
    m_recv,
    l_send,
    l_recv,
    u_send,
    u_recv,
):
    section = lax.axis_index("section")
    expert = lax.axis_index("expert")
    hops = choice_ref.shape[0]
    width, rows = x_ref.shape
    tile = row_tile(width)
    steps = n_expert - 1
    following = lax.rem(section + 1, n_section)
    previous = lax.rem(section + n_section - 1, n_section)

    def place(to_section, to_expert):
        return {"section": to_section, "expert": to_expert}

    loads = [
        pltpu.make_async_copy(source, target, load_sem.at[i])
        for i, (source, target) in enumerate(
            (
                (tokens_ref, x_ref),
                (down_ref, down_v),
                (up_ref, up_v),
                (weight_in_ref, weight_in_v),
                (weight_out_ref, weight_out_v),
            )
        )
    ]
    for load in loads:
        load.start()

    barrier = pltpu.get_barrier_semaphore()
    for target in (
        place(following, expert),
        place(previous, expert),
        place(section, lax.rem(expert + 1, n_expert)),
        place(section, lax.rem(expert + n_expert - 1, n_expert)),
        place(section, lax.rem(expert + 2, n_expert)),
    ):
        pl.semaphore_signal(barrier, inc=1, device_id=target, device_id_type=pl.DeviceIdType.MESH)

    before = (
        lax.broadcasted_iota(jnp.int32, (rows, rows), 0)
        < lax.broadcasted_iota(jnp.int32, (rows, rows), 1)
    ).astype(jnp.float32).astype(jnp.bfloat16)
    meta_own[...] = jnp.zeros_like(meta_own)
    for hop in range(hops):
        picks = choice_ref[hop]
        mix = router_ref[hop].astype(jnp.float32)
        here = (picks == 0).astype(jnp.float32)
        flag = jnp.max(here, axis=0, keepdims=True)
        position = jnp.dot(
            jnp.broadcast_to(flag, (16, rows)).astype(jnp.bfloat16),
            before,
            preferred_element_type=jnp.float32,
        )[:1]
        chosen = jnp.sum(here * mix, axis=0, keepdims=True)
        total = jnp.sum(mix, axis=0, keepdims=True)
        meta_own[hop, 0:1, :] = jnp.where(flag > 0.0, position, float(CAP))
        meta_own[hop, 1:2, :] = chosen / total

    for start in range(0, width, 128):
        stop = min(start + 128, width)
        piece = jnp.broadcast_to(gain_ref[0:1, start:stop], (128, stop - start))
        gain_col[start:stop, :] = piece.T

    pl.semaphore_wait(barrier, 5)

    def remote(source, target, send, recv, device):
        return pltpu.make_async_remote_copy(
            src_ref=source,
            dst_ref=target,
            send_sem=send,
            recv_sem=recv,
            device_id=device,
            device_id_type=pl.DeviceIdType.MESH,
        )

    def tiles(body):
        def step(i, carry):
            body(pl.ds(pl.multiple_of(i * tile, tile), tile))
            return carry

        lax.fori_loop(0, width // tile, step, 0)

    pieces = [(start, min(start + 768, width)) for start in range(0, width, 768)]

    def lane_tiles(start, stop):
        return [(at, min(at + 384, stop)) for at in range(start, stop, 384)]

    def stream_copy(hop, c):
        start, stop = pieces[c]
        return remote(
            x_ref.at[start:stop],
            arrived.at[hop, start:stop],
            x_send.at[hop, c],
            x_recv.at[hop, c],
            place(following, expert),
        )

    loads[0].wait()
    for c in range(len(pieces)):
        stream_copy(0, c).start()
    meta_copy = remote(meta_own, meta_in, m_send, m_recv, place(following, expert))
    meta_copy.start()
    loads[2].wait()
    up_copy = remote(up_v, up_previous, u_send, u_recv, place(following, expert))
    up_copy.start()

    def one_hot(meta, hop):
        slots = lax.broadcasted_iota(jnp.int32, (CAP, rows), 0).astype(jnp.float32)
        return jnp.where(slots == meta[hop, 0:1, :], 1.0, 0.0).astype(jnp.bfloat16)

    def select_rows(select, values):
        return lax.dot_general(
            select, values, (((1,), (1,)), ((), ())), preferred_element_type=jnp.float32
        )

    raw_rows[...] = select_rows(one_hot(meta_own, 0), x_ref[...])

    def settle(hop, send_on):
        spread = one_hot(meta_in, hop)
        share = meta_in[hop, 1:2, :]
        square_sum[...] = jnp.zeros_like(square_sum)
        for c, (first, last) in enumerate(pieces):
            stream_copy(hop, c).wait_send()
            for start, stop in lane_tiles(first, last):
                picked = lax.dot_general(
                    expert_in[hop, :, start:stop],
                    spread,
                    (((0,), (0,)), ((), ())),
                    preferred_element_type=jnp.float32,
                )
                moved = (
                    arrived[hop, start:stop, :].astype(jnp.float32) + share * picked
                ).astype(jnp.bfloat16)
                x_ref[start:stop, :] = moved
                if send_on:
                    values = moved.astype(jnp.float32)
                    square_sum[...] += jnp.sum(
                        (values * values).reshape((stop - start) // 8, 8, rows), axis=0
                    )
            if send_on:
                stream_copy(hop + 1, c).start()

    def expert_partial(block):
        gate = lax.dot_general(
            block, weight_in_v[0], (((1,), (1,)), ((), ())), preferred_element_type=jnp.float32
        )
        up = lax.dot_general(
            block, weight_in_v[1], (((1,), (1,)), ((), ())), preferred_element_type=jnp.float32
        )
        activated = (gate * jax.nn.sigmoid(1.702 * gate) * (up + 1.0)).astype(jnp.bfloat16)
        return jnp.dot(
            activated, weight_out_v[...], preferred_element_type=jnp.float32
        ).astype(jnp.bfloat16)

    def left_at(distance):
        return expert >= distance

    def right_at(distance):
        return expert + distance < n_expert

    def gather_send(hop, k, side):
        source = own_rows.at[hop] if k == 0 else gathered.at[hop, k - 1, side]
        step = 1 if side == LEFT else -1
        return remote(
            source,
            gathered.at[hop, k, side],
            ag_send.at[hop, k, side],
            ag_recv.at[hop, k, side],
            place(section, lax.rem(expert + step + n_expert, n_expert)),
        )

    def gather_sends(hop, k):
        return (
            (left_at(k) & right_at(1), gather_send(hop, k, LEFT)),
            (right_at(k) & left_at(1), gather_send(hop, k, RIGHT)),
        )

    def piece_of(c):
        return slice(c * ROWS, (c + 1) * ROWS)

    def partial_send(hop, k, side, c):
        away = -(k + 1) if side == LEFT else k + 1
        return remote(
            partials.at[k, side, piece_of(c)],
            returned.at[hop, k, 1 - side, piece_of(c)],
            rs_send.at[hop, k, side, c],
            rs_recv.at[hop, k, 1 - side, c],
            place(section, lax.rem(expert + away + n_expert, n_expert)),
        )

    def relay_send(hop, k, side, c):
        away = -1 if side == LEFT else 1
        return remote(
            partials.at[k, side, piece_of(c)],
            relayed.at[hop, k - 1, side, piece_of(c)],
            rs_send.at[hop, k, side, c],
            relay_recv.at[hop, k - 1, side, c],
            place(section, lax.rem(expert + away + n_expert, n_expert)),
        )

    def at_end(side):
        return expert == (n_expert - 1 if side == LEFT else 0)

    def beside_end(side):
        return expert == (n_expert - 2 if side == LEFT else 1)

    def sends_here(k, side):
        if k == 0:
            return on_side(side, 1)
        return (expert >= k + 2) if side == LEFT else (expert + k + 2 < n_expert)

    def on_side(side, distance):
        return left_at(distance) if side == LEFT else right_at(distance)

    def hop_body(hop, carry):
        raw = raw_rows[...]
        row_scale = lax.rsqrt(
            jnp.sum(raw * raw, axis=1, keepdims=True) * (1.0 / width) + 1e-05
        )
        own_rows[hop] = (raw * row_scale * gain_ref[...]).astype(jnp.bfloat16)
        for valid, copy in gather_sends(hop, 0):
            pl.when(valid)(copy.start)

        @pl.when(hop == 0)
        def _():
            square_sum[...] = jnp.zeros_like(square_sum)

            def first_squares(at):
                values = x_ref[at, :].astype(jnp.float32)
                square_sum[...] += jnp.sum(
                    (values * values).reshape(tile // 8, 8, rows), axis=0
                )

            tiles(first_squares)
            loads[1].wait()

        @pl.when(hop > 0)
        def _():
            settle(hop - 1, True)

        scale = lax.rsqrt(
            jnp.sum(square_sum[...], axis=0, keepdims=True) * (1.0 / width) + 1e-05
        )

        def normalise(at):
            gain = jnp.concatenate([gain_col[at, :]] * (rows // 128), axis=1)
            normed[at, :] = (x_ref[at, :].astype(jnp.float32) * scale * gain).astype(jnp.bfloat16)

        tiles(normalise)
        low_own[hop] = lax.dot_general(
            down_v[...], normed[...], (((0,), (0,)), ((), ())), preferred_element_type=jnp.float32
        ).astype(jnp.bfloat16)
        low_copy = remote(
            low_own.at[hop], low_in.at[hop], l_send.at[hop], l_recv.at[hop], place(following, expert)
        )
        low_copy.start()

        def take_and_forward(k):
            for side in (LEFT, RIGHT):
                pl.when(on_side(side, k + 1))(gather_send(hop, k, side).wait_recv)
            if k + 1 < steps:
                for valid, copy in gather_sends(hop, k + 1):
                    pl.when(valid)(copy.start)

        take_and_forward(0)

        @pl.when(hop == 0)
        def _():
            loads[3].wait()
            loads[4].wait()

        expert_sum[...] = expert_partial(own_rows[hop]).astype(jnp.float32)
        for k in range(steps):

            @pl.when(left_at(k + 1) | right_at(k + 1))
            def _(k=k):
                block = gathered[hop, k].reshape(2 * CAP, width)
                partials[k] = expert_partial(block).reshape(2, CAP, width)

            for side in (LEFT, RIGHT):
                valid = on_side(side, k + 1)
                straight = valid & jnp.logical_not(beside_end(side))
                if k > 0:
                    straight = straight & jnp.logical_not(at_end(side))

                    @pl.when(valid & at_end(side))
                    def _(k=k, side=side):
                        for c in range(CAP // ROWS):
                            relay_send(hop, k, side, c).start()

                @pl.when(straight)
                def _(k=k, side=side):
                    for c in range(CAP // ROWS):
                        partial_send(hop, k, side, c).start()

            if k + 1 < steps:
                take_and_forward(k + 1)

        for k in range(steps - 1):
            for side in (LEFT, RIGHT):

                @pl.when(on_side(side, k + 1) & beside_end(side))
                def _(k=k, side=side):
                    for c in range(CAP // ROWS):
                        relay_send(hop, k + 1, side, c).wait_recv()
                        at = piece_of(c)
                        partials[k, side, at] = (
                            partials[k, side, at].astype(jnp.float32)
                            + relayed[hop, k, side, at].astype(jnp.float32)
                        ).astype(jnp.bfloat16)
                        partial_send(hop, k, side, c).start()

        @pl.when(hop == 0)
        def _():
            meta_copy.wait()
            up_copy.wait()

        low_copy.wait()
        more = hop + 1 < hops

        def adapt(c):
            first, last = pieces[c]
            stream_copy(hop, c).wait_recv()
            for start, stop in lane_tiles(first, last):
                arrived[hop, start:stop, :] = (
                    arrived[hop, start:stop, :].astype(jnp.float32)
                    + jnp.dot(
                        up_previous[start:stop, :], low_in[hop], preferred_element_type=jnp.float32
                    )
                ).astype(jnp.bfloat16)

            @pl.when(more)
            def _():
                raw_rows[:, first:last] = select_rows(
                    one_hot(meta_own, hop + 1), arrived[hop, first:last, :]
                )

        for c in range(len(pieces) - 1):
            adapt(c)

        for k in range(steps):
            for side in (LEFT, RIGHT):

                @pl.when(sends_here(k, side))
                def _(k=k, side=side):
                    for c in range(CAP // ROWS):
                        partial_send(hop, k, 1 - side, c).wait_recv()
                    expert_sum[...] += returned[hop, k, side].astype(jnp.float32)

        expert_own[hop] = expert_sum[...].astype(jnp.bfloat16)
        expert_copy = remote(
            expert_own.at[hop],
            expert_in.at[hop],
            e_send.at[hop],
            e_recv.at[hop],
            place(following, expert),
        )
        expert_copy.start()
        adapt(len(pieces) - 1)

        for k in range(steps):
            for valid, copy in gather_sends(hop, k):
                pl.when(valid)(copy.wait_send)
            for side in (LEFT, RIGHT):
                for c in range(CAP // ROWS):
                    pl.when(on_side(side, k + 1))(partial_send(hop, k, side, c).wait_send)

        @pl.when(more)
        def _():
            chosen = one_hot(meta_own, hop + 1)
            meeting = select_rows(chosen, one_hot(meta_in, hop)).astype(jnp.bfloat16)
            share = jnp.sum(
                chosen.astype(jnp.float32) * meta_in[hop, 1:2, :], axis=1, keepdims=True
            )
            expert_copy.wait()
            picked = jnp.dot(meeting, expert_in[hop], preferred_element_type=jnp.float32)
            raw_rows[...] = (
                (raw_rows[...] + share * picked).astype(jnp.bfloat16).astype(jnp.float32)
            )

        @pl.when(hop + 1 == hops)
        def _():
            expert_copy.wait()

        return carry

    lax.fori_loop(0, hops, hop_body, 0)
    settle(hops - 1, False)


def body(
    n_section,
    n_expert,
    tokens,
    segment_norm_scale,
    expert_choice_table,
    router_weight_table,
    adapter_down_weight,
    adapter_up_weight,
    expert_gate_up_weight,
    expert_down_weight,
):
    rows, width = tokens.shape
    hops, _, top = expert_choice_table.shape
    rank = adapter_down_weight.shape[2]
    hid = expert_down_weight.shape[1]
    steps = n_expert - 1
    stream_pieces = pl.cdiv(width, 768)
    half = jnp.bfloat16
    full = jnp.float32
    block = (CAP, width)
    dma = pltpu.SemaphoreType.DMA
    flops = hops * (4 * rows * width * rank + 6 * n_expert * CAP * width * hid)
    out = pl.pallas_call(
        functools.partial(relay_kernel, n_section, n_expert),
        out_shape=jax.ShapeDtypeStruct((width, rows), half),
        in_specs=[
            pl.BlockSpec(memory_space=pl.ANY),
            pl.BlockSpec(memory_space=pltpu.VMEM),
            pl.BlockSpec(memory_space=pltpu.VMEM),
            pl.BlockSpec(memory_space=pltpu.VMEM),
            pl.BlockSpec(memory_space=pl.ANY),
            pl.BlockSpec(memory_space=pl.ANY),
            pl.BlockSpec(memory_space=pl.ANY),
            pl.BlockSpec(memory_space=pl.ANY),
        ],
        out_specs=pl.BlockSpec(memory_space=pltpu.VMEM),
        scratch_shapes=[
            pltpu.VMEM((width, rows), half),
            pltpu.VMEM((hops, width, rows), half),
            pltpu.VMEM((width, 128), full),
            pltpu.VMEM((8, rows), full),
            pltpu.VMEM((hops,) + block, half),
            pltpu.VMEM((hops, steps, 2) + block, half),
            pltpu.VMEM((steps, 2) + block, half),
            pltpu.VMEM((hops, steps, 2) + block, half),
            pltpu.VMEM((hops, steps - 1, 2) + block, half),
            pltpu.VMEM(block, full),
            pltpu.VMEM((hops,) + block, half),
            pltpu.VMEM((hops,) + block, half),
            pltpu.VMEM(block, full),
            pltpu.VMEM((hops, rank, rows), half),
            pltpu.VMEM((hops, rank, rows), half),
            pltpu.VMEM((width, rank), half),
            pltpu.VMEM((hops, 8, rows), full),
            pltpu.VMEM((hops, 8, rows), full),
            pltpu.VMEM((width, rank), half),
            pltpu.VMEM((width, rank), half),
            pltpu.VMEM((2, hid, width), half),
            pltpu.VMEM((hid, width), half),
            dma((5,)),
            dma((hops, steps, 2)),
            dma((hops, steps, 2)),
            dma((hops, steps, 2, CAP // ROWS)),
            dma((hops, steps, 2, CAP // ROWS)),
            dma((hops, steps - 1, 2, CAP // ROWS)),
            dma((hops, stream_pieces)),
            dma((hops, stream_pieces)),
            dma((hops,)),
            dma((hops,)),
            dma,
            dma,
            dma((hops,)),
            dma((hops,)),
            dma,
            dma,
        ],
        compiler_params=pltpu.CompilerParams(
            collective_id=0, has_side_effects=True, vmem_limit_bytes=60 * 2**20
        ),
        cost_estimate=pl.CostEstimate(
            flops=flops, bytes_accessed=16 * 2**20, transcendentals=hops * n_expert * CAP * hid
        ),
    )(
        tokens.T,
        segment_norm_scale,
        jnp.transpose(expert_choice_table, (0, 2, 1)),
        jnp.transpose(router_weight_table, (0, 2, 1)),
        adapter_down_weight[0],
        adapter_up_weight[0].T,
        jnp.transpose(expert_gate_up_weight[0], (1, 2, 0)),
        expert_down_weight[0],
    )
    return out.T


def solution(mesh):
    return jax.shard_map(
        functools.partial(body, mesh.shape["section"], mesh.shape["expert"]),
        mesh=mesh,
        in_specs=(
            P(("section", "expert"), None),
            P("section", None),
            P(None, ("section", "expert"), None),
            P(None, ("section", "expert"), None),
            P("section", None, None),
            P("section", None, None),
            P("section", None, None, "expert"),
            P("section", "expert", None),
        ),
        out_specs=P(("section", "expert"), None),
        check_vma=False,
    )
```

```python
import functools

import jax
import jax.numpy as jnp
from jax import lax
from jax.experimental import pallas as pl
from jax.experimental.pallas import tpu as pltpu
from jax.sharding import PartitionSpec as P

CAP = 48
ROWS = 16
LEFT, RIGHT = 0, 1


def row_tile(width):
    for tile in (320, 192, 64, 16):
        if width % tile == 0:
            return tile
    return width


def relay_kernel(
    n_section,
    n_expert,
    tokens_ref,
    gain_ref,
    choice_ref,
    router_ref,
    down_ref,
    up_ref,
    weight_in_ref,
    weight_out_ref,
    out_ref,
    last_sum_ref,
    last_meta_ref,
    x_ref,
    normed,
    arrived,
    gain_col,
    square_sum,
    own_rows,
    gathered,
    partials,
    returned,
    relayed,
    expert_sum,
    expert_own,
    expert_in,
    raw_rows,
    low_own,
    low_in,
    up_previous,
    meta_own,
    meta_in,
    down_v,
    up_v,
    weight_in_v,
    weight_out_v,
    load_sem,
    ag_send,
    ag_recv,
    rs_send,
    rs_recv,
    relay_recv,
    x_send,
    x_recv,
    e_send,
    e_recv,
    m_send,
    m_recv,
    l_send,
    l_recv,
    u_send,
    u_recv,
    out_sem,
):
    section = lax.axis_index("section")
    expert = lax.axis_index("expert")
    hops = choice_ref.shape[0]
    width, rows = x_ref.shape
    tile = row_tile(width)
    steps = n_expert - 1
    following = lax.rem(section + 1, n_section)
    previous = lax.rem(section + n_section - 1, n_section)

    def place(to_section, to_expert):
        return {"section": to_section, "expert": to_expert}

    loads = [
        pltpu.make_async_copy(source, target, load_sem.at[i])
        for i, (source, target) in enumerate(
            (
                (tokens_ref, x_ref),
                (down_ref, down_v),
                (up_ref, up_v),
                (weight_in_ref, weight_in_v),
                (weight_out_ref, weight_out_v),
            )
        )
    ]
    for load in loads:
        load.start()

    barrier = pltpu.get_barrier_semaphore()
    for target in (
        place(following, expert),
        place(previous, expert),
        place(section, lax.rem(expert + 1, n_expert)),
        place(section, lax.rem(expert + n_expert - 1, n_expert)),
        place(section, lax.rem(expert + 2, n_expert)),
    ):
        pl.semaphore_signal(barrier, inc=1, device_id=target, device_id_type=pl.DeviceIdType.MESH)

    before = (
        lax.broadcasted_iota(jnp.int32, (rows, rows), 0)
        < lax.broadcasted_iota(jnp.int32, (rows, rows), 1)
    ).astype(jnp.float32).astype(jnp.bfloat16)
    meta_own[...] = jnp.zeros_like(meta_own)
    for hop in range(hops):
        picks = choice_ref[hop]
        mix = router_ref[hop].astype(jnp.float32)
        here = (picks == 0).astype(jnp.float32)
        flag = jnp.max(here, axis=0, keepdims=True)
        position = jnp.dot(
            jnp.broadcast_to(flag, (16, rows)).astype(jnp.bfloat16),
            before,
            preferred_element_type=jnp.float32,
        )[:1]
        chosen = jnp.sum(here * mix, axis=0, keepdims=True)
        total = jnp.sum(mix, axis=0, keepdims=True)
        meta_own[hop, 0:1, :] = jnp.where(flag > 0.0, position, float(CAP))
        meta_own[hop, 1:2, :] = chosen / total

    pl.semaphore_wait(barrier, 5)

    def remote(source, target, send, recv, device):
        return pltpu.make_async_remote_copy(
            src_ref=source,
            dst_ref=target,
            send_sem=send,
            recv_sem=recv,
            device_id=device,
            device_id_type=pl.DeviceIdType.MESH,
        )

    def tiles(body):
        def step(i, carry):
            body(pl.ds(pl.multiple_of(i * tile, tile), tile))
            return carry

        lax.fori_loop(0, width // tile, step, 0)

    pieces = [(start, min(start + 768, width)) for start in range(0, width, 768)]

    def lane_tiles(start, stop):
        return [(at, min(at + 384, stop)) for at in range(start, stop, 384)]

    def stream_copy(hop, c):
        start, stop = pieces[c]
        return remote(
            x_ref.at[start:stop],
            arrived.at[hop, start:stop],
            x_send.at[hop, c],
            x_recv.at[hop, c],
            place(following, expert),
        )

    loads[0].wait()
    for c in range(len(pieces)):
        stream_copy(0, c).start()
    meta_copy = remote(meta_own, meta_in, m_send, m_recv, place(following, expert))
    meta_copy.start()
    loads[2].wait()
    up_copy = remote(up_v, up_previous, u_send, u_recv, place(following, expert))
    up_copy.start()

    def expert_copy(hop, c):
        at = slice(c * ROWS, (c + 1) * ROWS)
        return remote(
            expert_own.at[hop, at],
            expert_in.at[hop, at],
            e_send.at[hop, c],
            e_recv.at[hop, c],
            place(following, expert),
        )

    def one_hot(meta, hop):
        slots = lax.broadcasted_iota(jnp.int32, (CAP, rows), 0).astype(jnp.float32)
        return jnp.where(slots == meta[hop, 0:1, :], 1.0, 0.0).astype(jnp.bfloat16)

    def select_rows(select, values):
        return lax.dot_general(
            select, values, (((1,), (1,)), ((), ())), preferred_element_type=jnp.float32
        )

    raw_rows[...] = select_rows(one_hot(meta_own, 0), x_ref[...])

    def settle(hop):
        spread = one_hot(meta_in, hop)
        share = meta_in[hop, 1:2, :]
        square_sum[...] = jnp.zeros_like(square_sum)
        for c, (first, last) in enumerate(pieces):
            stream_copy(hop, c).wait_send()
            for start, stop in lane_tiles(first, last):
                picked = lax.dot_general(
                    expert_in[hop, :, start:stop],
                    spread,
                    (((0,), (0,)), ((), ())),
                    preferred_element_type=jnp.float32,
                )
                moved = (
                    arrived[hop, start:stop, :].astype(jnp.float32) + share * picked
                ).astype(jnp.bfloat16)
                x_ref[start:stop, :] = moved
                values = moved.astype(jnp.float32)
                square_sum[...] += jnp.sum(
                    (values * values).reshape((stop - start) // 8, 8, rows), axis=0
                )
            stream_copy(hop + 1, c).start()

    def write_out(c):
        start, stop = pieces[c]
        return pltpu.make_async_copy(
            arrived.at[hops - 1, start:stop], out_ref.at[start:stop], out_sem.at[c]
        )

    def expert_partial(block):
        gate = lax.dot_general(
            block, weight_in_v[0], (((1,), (1,)), ((), ())), preferred_element_type=jnp.float32
        )
        up = lax.dot_general(
            block, weight_in_v[1], (((1,), (1,)), ((), ())), preferred_element_type=jnp.float32
        )
        activated = (gate * jax.nn.sigmoid(1.702 * gate) * (up + 1.0)).astype(jnp.bfloat16)
        return jnp.dot(
            activated, weight_out_v[...], preferred_element_type=jnp.float32
        ).astype(jnp.bfloat16)

    def left_at(distance):
        return expert >= distance

    def right_at(distance):
        return expert + distance < n_expert

    def gather_send(hop, k, side):
        source = own_rows.at[hop] if k == 0 else gathered.at[hop, k - 1, side]
        step = 1 if side == LEFT else -1
        return remote(
            source,
            gathered.at[hop, k, side],
            ag_send.at[hop, k, side],
            ag_recv.at[hop, k, side],
            place(section, lax.rem(expert + step + n_expert, n_expert)),
        )

    def gather_sends(hop, k):
        return (
            (left_at(k) & right_at(1), gather_send(hop, k, LEFT)),
            (right_at(k) & left_at(1), gather_send(hop, k, RIGHT)),
        )

    def piece_of(c):
        return slice(c * ROWS, (c + 1) * ROWS)

    def partial_send(hop, k, side, c):
        away = -(k + 1) if side == LEFT else k + 1
        return remote(
            partials.at[k, side, piece_of(c)],
            returned.at[hop, k, 1 - side, piece_of(c)],
            rs_send.at[hop, k, side, c],
            rs_recv.at[hop, k, 1 - side, c],
            place(section, lax.rem(expert + away + n_expert, n_expert)),
        )

    def relay_send(hop, k, side, c):
        away = -1 if side == LEFT else 1
        return remote(
            partials.at[k, side, piece_of(c)],
            relayed.at[hop, k - 1, side, piece_of(c)],
            rs_send.at[hop, k, side, c],
            relay_recv.at[hop, k - 1, side, c],
            place(section, lax.rem(expert + away + n_expert, n_expert)),
        )

    def at_end(side):
        return expert == (n_expert - 1 if side == LEFT else 0)

    def beside_end(side):
        return expert == (n_expert - 2 if side == LEFT else 1)

    def sends_here(k, side):
        if k == 0:
            return on_side(side, 1)
        return (expert >= k + 2) if side == LEFT else (expert + k + 2 < n_expert)

    def on_side(side, distance):
        return left_at(distance) if side == LEFT else right_at(distance)

    def hop_body(hop, carry):
        raw = raw_rows[...]
        row_scale = lax.rsqrt(
            jnp.sum(raw * raw, axis=1, keepdims=True) * (1.0 / width) + 1e-05
        )
        own_rows[hop] = (raw * row_scale * gain_ref[...]).astype(jnp.bfloat16)
        for valid, copy in gather_sends(hop, 0):
            pl.when(valid)(copy.start)

        @pl.when(hop == 0)
        def _():
            square_sum[...] = jnp.zeros_like(square_sum)

            def first_squares(at):
                values = x_ref[at, :].astype(jnp.float32)
                square_sum[...] += jnp.sum(
                    (values * values).reshape(tile // 8, 8, rows), axis=0
                )

            tiles(first_squares)
            for start in range(0, width, 128):
                stop = min(start + 128, width)
                piece = jnp.broadcast_to(gain_ref[0:1, start:stop], (128, stop - start))
                gain_col[start:stop, :] = piece.T
            loads[1].wait()

        @pl.when(hop > 0)
        def _():
            settle(hop - 1)

        scale = lax.rsqrt(
            jnp.sum(square_sum[...], axis=0, keepdims=True) * (1.0 / width) + 1e-05
        )

        def normalise(at):
            gain = jnp.concatenate([gain_col[at, :]] * (rows // 128), axis=1)
            normed[at, :] = (x_ref[at, :].astype(jnp.float32) * scale * gain).astype(jnp.bfloat16)

        tiles(normalise)
        low_own[hop] = lax.dot_general(
            down_v[...], normed[...], (((0,), (0,)), ((), ())), preferred_element_type=jnp.float32
        ).astype(jnp.bfloat16)
        low_copy = remote(
            low_own.at[hop], low_in.at[hop], l_send.at[hop], l_recv.at[hop], place(following, expert)
        )
        low_copy.start()

        def take_and_forward(k):
            for side in (LEFT, RIGHT):
                pl.when(on_side(side, k + 1))(gather_send(hop, k, side).wait_recv)
            if k + 1 < steps:
                for valid, copy in gather_sends(hop, k + 1):
                    pl.when(valid)(copy.start)

        take_and_forward(0)

        @pl.when(hop == 0)
        def _():
            loads[3].wait()
            loads[4].wait()

        expert_sum[...] = expert_partial(own_rows[hop]).astype(jnp.float32)
        for k in range(steps):

            @pl.when(left_at(k + 1) | right_at(k + 1))
            def _(k=k):
                block = gathered[hop, k].reshape(2 * CAP, width)
                partials[k] = expert_partial(block).reshape(2, CAP, width)

            for side in (LEFT, RIGHT):
                valid = on_side(side, k + 1)
                straight = valid & jnp.logical_not(beside_end(side))
                if k > 0:
                    straight = straight & jnp.logical_not(at_end(side))

                    @pl.when(valid & at_end(side))
                    def _(k=k, side=side):
                        for c in range(CAP // ROWS):
                            relay_send(hop, k, side, c).start()

                @pl.when(straight)
                def _(k=k, side=side):
                    for c in range(CAP // ROWS):
                        partial_send(hop, k, side, c).start()

            if k + 1 < steps:
                take_and_forward(k + 1)

        for k in range(steps - 1):
            for side in (LEFT, RIGHT):

                @pl.when(on_side(side, k + 1) & beside_end(side))
                def _(k=k, side=side):
                    for c in range(CAP // ROWS):
                        relay_send(hop, k + 1, side, c).wait_recv()
                        at = piece_of(c)
                        partials[k, side, at] = (
                            partials[k, side, at].astype(jnp.float32)
                            + relayed[hop, k, side, at].astype(jnp.float32)
                        ).astype(jnp.bfloat16)
                        partial_send(hop, k, side, c).start()

        @pl.when(hop == 0)
        def _():
            meta_copy.wait()
            up_copy.wait()

        low_copy.wait()
        more = hop + 1 < hops

        def adapt(c):
            first, last = pieces[c]
            stream_copy(hop, c).wait_recv()
            for start, stop in lane_tiles(first, last):
                arrived[hop, start:stop, :] = (
                    arrived[hop, start:stop, :].astype(jnp.float32)
                    + jnp.dot(
                        up_previous[start:stop, :], low_in[hop], preferred_element_type=jnp.float32
                    )
                ).astype(jnp.bfloat16)

            @pl.when(more)
            def _():
                raw_rows[:, first:last] = select_rows(
                    one_hot(meta_own, hop + 1), arrived[hop, first:last, :]
                )

            @pl.when(hop + 1 == hops)
            def _():
                write_out(c).start()

        for c in range(len(pieces) - 1):
            adapt(c)

        for c in range(CAP // ROWS):
            at = piece_of(c)
            for k in range(steps):
                for side in (LEFT, RIGHT):

                    @pl.when(sends_here(k, side))
                    def _(k=k, side=side, c=c, at=at):
                        partial_send(hop, k, 1 - side, c).wait_recv()
                        expert_sum[at] += returned[hop, k, side, at].astype(jnp.float32)

            expert_own[hop, at] = expert_sum[at].astype(jnp.bfloat16)
            expert_copy(hop, c).start()

        adapt(len(pieces) - 1)

        for k in range(steps):
            for valid, copy in gather_sends(hop, k):
                pl.when(valid)(copy.wait_send)
            for side in (LEFT, RIGHT):
                for c in range(CAP // ROWS):
                    pl.when(on_side(side, k + 1))(partial_send(hop, k, side, c).wait_send)

        @pl.when(more)
        def _():
            chosen = one_hot(meta_own, hop + 1)
            meeting = select_rows(chosen, one_hot(meta_in, hop)).astype(jnp.bfloat16)
            share = jnp.sum(
                chosen.astype(jnp.float32) * meta_in[hop, 1:2, :], axis=1, keepdims=True
            )
            for c in range(CAP // ROWS):
                expert_copy(hop, c).wait()
            picked = jnp.dot(meeting, expert_in[hop], preferred_element_type=jnp.float32)
            raw_rows[...] = (
                (raw_rows[...] + share * picked).astype(jnp.bfloat16).astype(jnp.float32)
            )

        @pl.when(hop + 1 == hops)
        def _():
            for c in range(CAP // ROWS):
                expert_copy(hop, c).wait()

        return carry

    lax.fori_loop(0, hops, hop_body, 0)
    last_sum_ref[...] = expert_in[hops - 1]
    last_meta_ref[...] = meta_in[hops - 1]
    for c in range(len(pieces)):
        stream_copy(hops - 1, c).wait_send()
        write_out(c).wait()


def last_kernel(adapted_ref, expert_ref, meta_ref, out_ref):
    rows = out_ref.shape[1]
    slots = lax.broadcasted_iota(jnp.int32, (CAP, rows), 0).astype(jnp.float32)
    spread = jnp.where(slots == meta_ref[0:1, :], 1.0, 0.0).astype(jnp.bfloat16)
    picked = lax.dot_general(
        expert_ref[...], spread, (((0,), (0,)), ((), ())), preferred_element_type=jnp.float32
    )
    out_ref[...] = (
        adapted_ref[...].astype(jnp.float32) + meta_ref[1:2, :] * picked
    ).astype(out_ref.dtype)


def body(
    n_section,
    n_expert,
    tokens,
    segment_norm_scale,
    expert_choice_table,
    router_weight_table,
    adapter_down_weight,
    adapter_up_weight,
    expert_gate_up_weight,
    expert_down_weight,
):
    rows, width = tokens.shape
    hops, _, top = expert_choice_table.shape
    rank = adapter_down_weight.shape[2]
    hid = expert_down_weight.shape[1]
    steps = n_expert - 1
    stream_pieces = pl.cdiv(width, 768)
    half = jnp.bfloat16
    full = jnp.float32
    block = (CAP, width)
    dma = pltpu.SemaphoreType.DMA
    flops = hops * (4 * rows * width * rank + 6 * n_expert * CAP * width * hid)
    adapted, last_sum, last_meta = pl.pallas_call(
        functools.partial(relay_kernel, n_section, n_expert),
        out_shape=(
            jax.ShapeDtypeStruct((width, rows), half),
            jax.ShapeDtypeStruct(block, half),
            jax.ShapeDtypeStruct((8, rows), full),
        ),
        in_specs=[
            pl.BlockSpec(memory_space=pl.ANY),
            pl.BlockSpec(memory_space=pltpu.VMEM),
            pl.BlockSpec(memory_space=pltpu.VMEM),
            pl.BlockSpec(memory_space=pltpu.VMEM),
            pl.BlockSpec(memory_space=pl.ANY),
            pl.BlockSpec(memory_space=pl.ANY),
            pl.BlockSpec(memory_space=pl.ANY),
            pl.BlockSpec(memory_space=pl.ANY),
        ],
        out_specs=(
            pl.BlockSpec(memory_space=pl.ANY),
            pl.BlockSpec(memory_space=pltpu.VMEM),
            pl.BlockSpec(memory_space=pltpu.VMEM),
        ),
        scratch_shapes=[
            pltpu.VMEM((width, rows), half),
            pltpu.VMEM((width, rows), half),
            pltpu.VMEM((hops, width, rows), half),
            pltpu.VMEM((width, 128), full),
            pltpu.VMEM((8, rows), full),
            pltpu.VMEM((hops,) + block, half),
            pltpu.VMEM((hops, steps, 2) + block, half),
            pltpu.VMEM((steps, 2) + block, half),
            pltpu.VMEM((hops, steps, 2) + block, half),
            pltpu.VMEM((hops, steps - 1, 2) + block, half),
            pltpu.VMEM(block, full),
            pltpu.VMEM((hops,) + block, half),
            pltpu.VMEM((hops,) + block, half),
            pltpu.VMEM(block, full),
            pltpu.VMEM((hops, rank, rows), half),
            pltpu.VMEM((hops, rank, rows), half),
            pltpu.VMEM((width, rank), half),
            pltpu.VMEM((hops, 8, rows), full),
            pltpu.VMEM((hops, 8, rows), full),
            pltpu.VMEM((width, rank), half),
            pltpu.VMEM((width, rank), half),
            pltpu.VMEM((2, hid, width), half),
            pltpu.VMEM((hid, width), half),
            dma((5,)),
            dma((hops, steps, 2)),
            dma((hops, steps, 2)),
            dma((hops, steps, 2, CAP // ROWS)),
            dma((hops, steps, 2, CAP // ROWS)),
            dma((hops, steps - 1, 2, CAP // ROWS)),
            dma((hops, stream_pieces)),
            dma((hops, stream_pieces)),
            dma((hops, CAP // ROWS)),
            dma((hops, CAP // ROWS)),
            dma,
            dma,
            dma((hops,)),
            dma((hops,)),
            dma,
            dma,
            dma((stream_pieces,)),
        ],
        compiler_params=pltpu.CompilerParams(
            collective_id=0, has_side_effects=True, vmem_limit_bytes=60 * 2**20
        ),
        cost_estimate=pl.CostEstimate(
            flops=flops, bytes_accessed=16 * 2**20, transcendentals=hops * n_expert * CAP * hid
        ),
    )(
        tokens.T,
        segment_norm_scale,
        jnp.transpose(expert_choice_table, (0, 2, 1)),
        jnp.transpose(router_weight_table, (0, 2, 1)),
        adapter_down_weight[0],
        adapter_up_weight[0].T,
        jnp.transpose(expert_gate_up_weight[0], (1, 2, 0)),
        expert_down_weight[0],
    )
    lanes = 384
    out = pl.pallas_call(
        last_kernel,
        out_shape=jax.ShapeDtypeStruct((width, rows), half),
        grid=(pl.cdiv(width, lanes),),
        in_specs=[
            pl.BlockSpec((lanes, rows), lambda i: (i, 0)),
            pl.BlockSpec((CAP, lanes), lambda i: (0, i)),
            pl.BlockSpec((8, rows), lambda i: (0, 0)),
        ],
        out_specs=pl.BlockSpec((lanes, rows), lambda i: (i, 0)),
        cost_estimate=pl.CostEstimate(
            flops=2 * CAP * width * rows, bytes_accessed=4 * width * rows, transcendentals=0
        ),
    )(adapted, last_sum, last_meta)
    return out.T


def solution(mesh):
    return jax.shard_map(
        functools.partial(body, mesh.shape["section"], mesh.shape["expert"]),
        mesh=mesh,
        in_specs=(
            P(("section", "expert"), None),
            P("section", None),
            P(None, ("section", "expert"), None),
            P(None, ("section", "expert"), None),
            P("section", None, None),
            P("section", None, None),
            P("section", None, None, "expert"),
            P("section", "expert", None),
        ),
        out_specs=P(("section", "expert"), None),
        check_vma=False,
    )
```

```python
import functools

import jax
import jax.numpy as jnp
from jax import lax
from jax.experimental import pallas as pl
from jax.experimental.pallas import tpu as pltpu
from jax.sharding import PartitionSpec as P

CAP = 48
ROWS = 16
LEFT, RIGHT = 0, 1


def row_tile(width):
    for tile in (320, 192, 64, 16):
        if width % tile == 0:
            return tile
    return width


def relay_kernel(
    n_section,
    n_expert,
    tokens_ref,
    gain_ref,
    choice_ref,
    router_ref,
    down_ref,
    up_ref,
    weight_in_ref,
    weight_out_ref,
    out_ref,
    last_sum_ref,
    last_meta_ref,
    x_ref,
    normed,
    arrived,
    gain_col,
    square_sum,
    own_rows,
    gathered,
    partials,
    returned,
    relayed,
    expert_sum,
    expert_own,
    expert_in,
    raw_rows,
    low_own,
    low_in,
    up_previous,
    meta_own,
    meta_in,
    down_v,
    up_v,
    weight_in_v,
    weight_out_v,
    load_sem,
    ag_send,
    ag_recv,
    rs_send,
    rs_recv,
    relay_recv,
    x_send,
    x_recv,
    e_send,
    e_recv,
    m_send,
    m_recv,
    l_send,
    l_recv,
    u_send,
    u_recv,
    out_sem,
):
    section = lax.axis_index("section")
    expert = lax.axis_index("expert")
    hops = choice_ref.shape[0]
    width, rows = x_ref.shape
    tile = row_tile(width)
    steps = n_expert - 1
    following = lax.rem(section + 1, n_section)
    previous = lax.rem(section + n_section - 1, n_section)

    def place(to_section, to_expert):
        return {"section": to_section, "expert": to_expert}

    loads = [
        pltpu.make_async_copy(source, target, load_sem.at[i])
        for i, (source, target) in enumerate(
            (
                (tokens_ref, x_ref),
                (down_ref, down_v),
                (up_ref, up_v),
                (weight_in_ref, weight_in_v),
                (weight_out_ref, weight_out_v),
            )
        )
    ]
    for load in loads:
        load.start()

    barrier = pltpu.get_barrier_semaphore()
    for target in (
        place(following, expert),
        place(previous, expert),
        place(section, lax.rem(expert + 1, n_expert)),
        place(section, lax.rem(expert + n_expert - 1, n_expert)),
        place(section, lax.rem(expert + 2, n_expert)),
    ):
        pl.semaphore_signal(barrier, inc=1, device_id=target, device_id_type=pl.DeviceIdType.MESH)

    pl.semaphore_wait(barrier, 5)

    def remote(source, target, send, recv, device):
        return pltpu.make_async_remote_copy(
            src_ref=source,
            dst_ref=target,
            send_sem=send,
            recv_sem=recv,
            device_id=device,
            device_id_type=pl.DeviceIdType.MESH,
        )

    def tiles(body):
        def step(i, carry):
            body(pl.ds(pl.multiple_of(i * tile, tile), tile))
            return carry

        lax.fori_loop(0, width // tile, step, 0)

    pieces = [(start, min(start + 768, width)) for start in range(0, width, 768)]

    def lane_tiles(start, stop):
        return [(at, min(at + 384, stop)) for at in range(start, stop, 384)]

    def stream_copy(hop, c):
        start, stop = pieces[c]
        return remote(
            x_ref.at[start:stop],
            arrived.at[hop, start:stop],
            x_send.at[hop, c],
            x_recv.at[hop, c],
            place(following, expert),
        )

    loads[0].wait()
    stream_copy(0, 0).start()
    loads[2].wait()
    first_rows = pieces[0][1]
    up_copy = remote(
        up_v.at[0:first_rows], up_previous, u_send, u_recv, place(following, expert)
    )
    up_copy.start()

    before = (
        lax.broadcasted_iota(jnp.int32, (rows, rows), 0)
        < lax.broadcasted_iota(jnp.int32, (rows, rows), 1)
    ).astype(jnp.float32).astype(jnp.bfloat16)
    meta_own[...] = jnp.zeros_like(meta_own)
    for hop in range(hops):
        picks = choice_ref[hop]
        mix = router_ref[hop].astype(jnp.float32)
        here = (picks == 0).astype(jnp.float32)
        flag = jnp.max(here, axis=0, keepdims=True)
        position = jnp.dot(
            jnp.broadcast_to(flag, (16, rows)).astype(jnp.bfloat16),
            before,
            preferred_element_type=jnp.float32,
        )[:1]
        chosen = jnp.sum(here * mix, axis=0, keepdims=True)
        total = jnp.sum(mix, axis=0, keepdims=True)
        meta_own[hop, 0:1, :] = jnp.where(flag > 0.0, position, float(CAP))
        meta_own[hop, 1:2, :] = chosen / total

    meta_copy = remote(meta_own, meta_in, m_send, m_recv, place(following, expert))
    meta_copy.start()

    def expert_copy(hop, c):
        at = slice(c * ROWS, (c + 1) * ROWS)
        return remote(
            expert_own.at[hop, at],
            expert_in.at[hop, at],
            e_send.at[hop, c],
            e_recv.at[hop, c],
            place(following, expert),
        )

    def add_adapter(rows_ref, up_rows, low):
        rows_ref[...] = (
            rows_ref[...].astype(jnp.float32)
            + jnp.dot(up_rows, low, preferred_element_type=jnp.float32)
        ).astype(jnp.bfloat16)

    def one_hot(meta, hop):
        slots = lax.broadcasted_iota(jnp.int32, (CAP, rows), 0).astype(jnp.float32)
        return jnp.where(slots == meta[hop, 0:1, :], 1.0, 0.0).astype(jnp.bfloat16)

    def select_rows(select, values):
        return lax.dot_general(
            select, values, (((1,), (1,)), ((), ())), preferred_element_type=jnp.float32
        )

    raw_rows[...] = select_rows(one_hot(meta_own, 0), x_ref[...])

    def settle(hop):
        spread = one_hot(meta_in, hop)
        share = meta_in[hop, 1:2, :]
        square_sum[...] = jnp.zeros_like(square_sum)
        for c, (first, last) in enumerate(pieces):
            stream_copy(hop, c).wait_send()
            for start, stop in lane_tiles(first, last):
                picked = lax.dot_general(
                    expert_in[hop, :, start:stop],
                    spread,
                    (((0,), (0,)), ((), ())),
                    preferred_element_type=jnp.float32,
                )
                moved = (
                    arrived[hop, start:stop, :].astype(jnp.float32) + share * picked
                ).astype(jnp.bfloat16)
                x_ref[start:stop, :] = moved
                values = moved.astype(jnp.float32)
                square_sum[...] += jnp.sum(
                    (values * values).reshape((stop - start) // 8, 8, rows), axis=0
                )
            if c == 0:
                stream_copy(hop + 1, c).start()

    def write_out(c):
        start, stop = pieces[c]
        return pltpu.make_async_copy(
            arrived.at[hops - 1, start:stop], out_ref.at[start:stop], out_sem.at[c]
        )

    def expert_partial(block):
        gate = lax.dot_general(
            block, weight_in_v[0], (((1,), (1,)), ((), ())), preferred_element_type=jnp.float32
        )
        up = lax.dot_general(
            block, weight_in_v[1], (((1,), (1,)), ((), ())), preferred_element_type=jnp.float32
        )
        activated = (gate * jax.nn.sigmoid(1.702 * gate) * (up + 1.0)).astype(jnp.bfloat16)
        return jnp.dot(
            activated, weight_out_v[...], preferred_element_type=jnp.float32
        ).astype(jnp.bfloat16)

    def left_at(distance):
        return expert >= distance

    def right_at(distance):
        return expert + distance < n_expert

    def gather_send(hop, k, side):
        source = own_rows.at[hop] if k == 0 else gathered.at[hop, k - 1, side]
        step = 1 if side == LEFT else -1
        return remote(
            source,
            gathered.at[hop, k, side],
            ag_send.at[hop, k, side],
            ag_recv.at[hop, k, side],
            place(section, lax.rem(expert + step + n_expert, n_expert)),
        )

    def gather_sends(hop, k):
        return (
            (left_at(k) & right_at(1), gather_send(hop, k, LEFT)),
            (right_at(k) & left_at(1), gather_send(hop, k, RIGHT)),
        )

    def piece_of(c):
        return slice(c * ROWS, (c + 1) * ROWS)

    def partial_send(hop, k, side, c):
        away = -(k + 1) if side == LEFT else k + 1
        return remote(
            partials.at[k, side, piece_of(c)],
            returned.at[hop, k, 1 - side, piece_of(c)],
            rs_send.at[hop, k, side, c],
            rs_recv.at[hop, k, 1 - side, c],
            place(section, lax.rem(expert + away + n_expert, n_expert)),
        )

    def relay_send(hop, k, side, c):
        away = -1 if side == LEFT else 1
        return remote(
            partials.at[k, side, piece_of(c)],
            relayed.at[hop, k - 1, side, piece_of(c)],
            rs_send.at[hop, k, side, c],
            relay_recv.at[hop, k - 1, side, c],
            place(section, lax.rem(expert + away + n_expert, n_expert)),
        )

    def at_end(side):
        return expert == (n_expert - 1 if side == LEFT else 0)

    def beside_end(side):
        return expert == (n_expert - 2 if side == LEFT else 1)

    def sends_here(k, side):
        if k == 0:
            return on_side(side, 1)
        return (expert >= k + 2) if side == LEFT else (expert + k + 2 < n_expert)

    def on_side(side, distance):
        return left_at(distance) if side == LEFT else right_at(distance)

    def hop_body(hop, carry):
        raw = raw_rows[...]
        row_scale = lax.rsqrt(
            jnp.sum(raw * raw, axis=1, keepdims=True) * (1.0 / width) + 1e-05
        )
        own_rows[hop] = (raw * row_scale * gain_ref[...]).astype(jnp.bfloat16)
        for valid, copy in gather_sends(hop, 0):
            pl.when(valid)(copy.start)

        @pl.when(hop == 0)
        def _():
            square_sum[...] = jnp.zeros_like(square_sum)

            def first_squares(at):
                values = x_ref[at, :].astype(jnp.float32)
                square_sum[...] += jnp.sum(
                    (values * values).reshape(tile // 8, 8, rows), axis=0
                )

            tiles(first_squares)
            for start in range(0, width, 128):
                stop = min(start + 128, width)
                piece = jnp.broadcast_to(gain_ref[0:1, start:stop], (128, stop - start))
                gain_col[start:stop, :] = piece.T
            loads[1].wait()

        @pl.when(hop > 0)
        def _():
            settle(hop - 1)

        scale = lax.rsqrt(
            jnp.sum(square_sum[...], axis=0, keepdims=True) * (1.0 / width) + 1e-05
        )

        def normalise(at):
            gain = jnp.concatenate([gain_col[at, :]] * (rows // 128), axis=1)
            normed[at, :] = (x_ref[at, :].astype(jnp.float32) * scale * gain).astype(jnp.bfloat16)

        tiles(normalise)
        low_own[hop] = lax.dot_general(
            down_v[...], normed[...], (((0,), (0,)), ((), ())), preferred_element_type=jnp.float32
        ).astype(jnp.bfloat16)
        low_copy = remote(
            low_own.at[hop], low_in.at[hop], l_send.at[hop], l_recv.at[hop], place(following, expert)
        )
        low_copy.start()

        def take_and_forward(k):
            for side in (LEFT, RIGHT):
                pl.when(on_side(side, k + 1))(gather_send(hop, k, side).wait_recv)
            if k + 1 < steps:
                for valid, copy in gather_sends(hop, k + 1):
                    pl.when(valid)(copy.start)

        for c in range(1, len(pieces)):
            for start, stop in lane_tiles(*pieces[c]):
                add_adapter(x_ref.at[start:stop], up_v[start:stop, :], low_own[hop])
            stream_copy(hop, c).start()
            if c == 1:
                take_and_forward(0)

        @pl.when(hop == 0)
        def _():
            loads[3].wait()
            loads[4].wait()

        expert_sum[...] = expert_partial(own_rows[hop]).astype(jnp.float32)
        for k in range(steps):

            @pl.when(left_at(k + 1) | right_at(k + 1))
            def _(k=k):
                block = gathered[hop, k].reshape(2 * CAP, width)
                partials[k] = expert_partial(block).reshape(2, CAP, width)

            for side in (LEFT, RIGHT):
                valid = on_side(side, k + 1)
                straight = valid & jnp.logical_not(beside_end(side))
                if k > 0:
                    straight = straight & jnp.logical_not(at_end(side))

                    @pl.when(valid & at_end(side))
                    def _(k=k, side=side):
                        for c in range(CAP // ROWS):
                            relay_send(hop, k, side, c).start()

                @pl.when(straight)
                def _(k=k, side=side):
                    for c in range(CAP // ROWS):
                        partial_send(hop, k, side, c).start()

            if k + 1 < steps:
                take_and_forward(k + 1)

        for k in range(steps - 1):
            for side in (LEFT, RIGHT):

                @pl.when(on_side(side, k + 1) & beside_end(side))
                def _(k=k, side=side):
                    for c in range(CAP // ROWS):
                        relay_send(hop, k + 1, side, c).wait_recv()
                        at = piece_of(c)
                        partials[k, side, at] = (
                            partials[k, side, at].astype(jnp.float32)
                            + relayed[hop, k, side, at].astype(jnp.float32)
                        ).astype(jnp.bfloat16)
                        partial_send(hop, k, side, c).start()

        @pl.when(hop == 0)
        def _():
            meta_copy.wait()
            up_copy.wait()

        low_copy.wait()
        more = hop + 1 < hops

        def adapt(c):
            first, last = pieces[c]
            stream_copy(hop, c).wait_recv()
            if c == 0:
                for start, stop in lane_tiles(first, last):
                    add_adapter(
                        arrived.at[hop, start:stop], up_previous[start:stop, :], low_in[hop]
                    )

            @pl.when(more)
            def _():
                raw_rows[:, first:last] = select_rows(
                    one_hot(meta_own, hop + 1), arrived[hop, first:last, :]
                )

            @pl.when(hop + 1 == hops)
            def _():
                write_out(c).start()

        for c in range(len(pieces) - 1):
            adapt(c)

        for c in range(CAP // ROWS):
            at = piece_of(c)
            for k in range(steps):
                for side in (LEFT, RIGHT):

                    @pl.when(sends_here(k, side))
                    def _(k=k, side=side, c=c, at=at):
                        partial_send(hop, k, 1 - side, c).wait_recv()
                        expert_sum[at] += returned[hop, k, side, at].astype(jnp.float32)

            expert_own[hop, at] = expert_sum[at].astype(jnp.bfloat16)
            expert_copy(hop, c).start()

        adapt(len(pieces) - 1)

        for k in range(steps):
            for valid, copy in gather_sends(hop, k):
                pl.when(valid)(copy.wait_send)
            for side in (LEFT, RIGHT):
                for c in range(CAP // ROWS):
                    pl.when(on_side(side, k + 1))(partial_send(hop, k, side, c).wait_send)

        @pl.when(more)
        def _():
            chosen = one_hot(meta_own, hop + 1)
            meeting = select_rows(chosen, one_hot(meta_in, hop)).astype(jnp.bfloat16)
            share = jnp.sum(
                chosen.astype(jnp.float32) * meta_in[hop, 1:2, :], axis=1, keepdims=True
            )
            for c in range(CAP // ROWS):
                expert_copy(hop, c).wait()
            picked = jnp.dot(meeting, expert_in[hop], preferred_element_type=jnp.float32)
            raw_rows[...] = (
                (raw_rows[...] + share * picked).astype(jnp.bfloat16).astype(jnp.float32)
            )

        @pl.when(hop + 1 == hops)
        def _():
            for c in range(CAP // ROWS):
                expert_copy(hop, c).wait()

        return carry

    lax.fori_loop(0, hops, hop_body, 0)
    last_sum_ref[...] = expert_in[hops - 1]
    last_meta_ref[...] = meta_in[hops - 1]
    for c in range(len(pieces)):
        stream_copy(hops - 1, c).wait_send()
        write_out(c).wait()


def last_kernel(adapted_ref, expert_ref, meta_ref, out_ref):
    rows = out_ref.shape[1]
    slots = lax.broadcasted_iota(jnp.int32, (CAP, rows), 0).astype(jnp.float32)
    spread = jnp.where(slots == meta_ref[0:1, :], 1.0, 0.0).astype(jnp.bfloat16)
    picked = lax.dot_general(
        expert_ref[...], spread, (((0,), (0,)), ((), ())), preferred_element_type=jnp.float32
    )
    out_ref[...] = (
        adapted_ref[...].astype(jnp.float32) + meta_ref[1:2, :] * picked
    ).astype(out_ref.dtype)


def body(
    n_section,
    n_expert,
    tokens,
    segment_norm_scale,
    expert_choice_table,
    router_weight_table,
    adapter_down_weight,
    adapter_up_weight,
    expert_gate_up_weight,
    expert_down_weight,
):
    rows, width = tokens.shape
    hops, _, top = expert_choice_table.shape
    rank = adapter_down_weight.shape[2]
    hid = expert_down_weight.shape[1]
    steps = n_expert - 1
    stream_pieces = pl.cdiv(width, 768)
    half = jnp.bfloat16
    full = jnp.float32
    block = (CAP, width)
    dma = pltpu.SemaphoreType.DMA
    flops = hops * (4 * rows * width * rank + 6 * n_expert * CAP * width * hid)
    adapted, last_sum, last_meta = pl.pallas_call(
        functools.partial(relay_kernel, n_section, n_expert),
        out_shape=(
            jax.ShapeDtypeStruct((width, rows), half),
            jax.ShapeDtypeStruct(block, half),
            jax.ShapeDtypeStruct((8, rows), full),
        ),
        in_specs=[
            pl.BlockSpec(memory_space=pl.ANY),
            pl.BlockSpec(memory_space=pltpu.VMEM),
            pl.BlockSpec(memory_space=pltpu.VMEM),
            pl.BlockSpec(memory_space=pltpu.VMEM),
            pl.BlockSpec(memory_space=pl.ANY),
            pl.BlockSpec(memory_space=pl.ANY),
            pl.BlockSpec(memory_space=pl.ANY),
            pl.BlockSpec(memory_space=pl.ANY),
        ],
        out_specs=(
            pl.BlockSpec(memory_space=pl.ANY),
            pl.BlockSpec(memory_space=pltpu.VMEM),
            pl.BlockSpec(memory_space=pltpu.VMEM),
        ),
        scratch_shapes=[
            pltpu.VMEM((width, rows), half),
            pltpu.VMEM((width, rows), half),
            pltpu.VMEM((hops, width, rows), half),
            pltpu.VMEM((width, 128), full),
            pltpu.VMEM((8, rows), full),
            pltpu.VMEM((hops,) + block, half),
            pltpu.VMEM((hops, steps, 2) + block, half),
            pltpu.VMEM((steps, 2) + block, half),
            pltpu.VMEM((hops, steps, 2) + block, half),
            pltpu.VMEM((hops, steps - 1, 2) + block, half),
            pltpu.VMEM(block, full),
            pltpu.VMEM((hops,) + block, half),
            pltpu.VMEM((hops,) + block, half),
            pltpu.VMEM(block, full),
            pltpu.VMEM((hops, rank, rows), half),
            pltpu.VMEM((hops, rank, rows), half),
            pltpu.VMEM((min(width, 768), rank), half),
            pltpu.VMEM((hops, 8, rows), full),
            pltpu.VMEM((hops, 8, rows), full),
            pltpu.VMEM((width, rank), half),
            pltpu.VMEM((width, rank), half),
            pltpu.VMEM((2, hid, width), half),
            pltpu.VMEM((hid, width), half),
            dma((5,)),
            dma((hops, steps, 2)),
            dma((hops, steps, 2)),
            dma((hops, steps, 2, CAP // ROWS)),
            dma((hops, steps, 2, CAP // ROWS)),
            dma((hops, steps - 1, 2, CAP // ROWS)),
            dma((hops, stream_pieces)),
            dma((hops, stream_pieces)),
            dma((hops, CAP // ROWS)),
            dma((hops, CAP // ROWS)),
            dma,
            dma,
            dma((hops,)),
            dma((hops,)),
            dma,
            dma,
            dma((stream_pieces,)),
        ],
        compiler_params=pltpu.CompilerParams(
            collective_id=0, has_side_effects=True, vmem_limit_bytes=60 * 2**20
        ),
        cost_estimate=pl.CostEstimate(
            flops=flops, bytes_accessed=16 * 2**20, transcendentals=hops * n_expert * CAP * hid
        ),
    )(
        tokens.T,
        segment_norm_scale,
        jnp.transpose(expert_choice_table, (0, 2, 1)),
        jnp.transpose(router_weight_table, (0, 2, 1)),
        adapter_down_weight[0],
        adapter_up_weight[0].T,
        jnp.transpose(expert_gate_up_weight[0], (1, 2, 0)),
        expert_down_weight[0],
    )
    lanes = 768
    out = pl.pallas_call(
        last_kernel,
        out_shape=jax.ShapeDtypeStruct((width, rows), half),
        grid=(pl.cdiv(width, lanes),),
        in_specs=[
            pl.BlockSpec((lanes, rows), lambda i: (i, 0)),
            pl.BlockSpec((CAP, lanes), lambda i: (0, i)),
            pl.BlockSpec((8, rows), lambda i: (0, 0)),
        ],
        out_specs=pl.BlockSpec((lanes, rows), lambda i: (i, 0)),
        cost_estimate=pl.CostEstimate(
            flops=2 * CAP * width * rows, bytes_accessed=4 * width * rows, transcendentals=0
        ),
    )(adapted, last_sum, last_meta)
    return out.T


def solution(mesh):
    return jax.shard_map(
        functools.partial(body, mesh.shape["section"], mesh.shape["expert"]),
        mesh=mesh,
        in_specs=(
            P(("section", "expert"), None),
            P("section", None),
            P(None, ("section", "expert"), None),
            P(None, ("section", "expert"), None),
            P("section", None, None),
            P("section", None, None),
            P("section", None, None, "expert"),
            P("section", "expert", None),
        ),
        out_specs=P(("section", "expert"), None),
        check_vma=False,
    )
```

```python
import functools

import jax
import jax.numpy as jnp
from jax import lax
from jax.experimental import pallas as pl
from jax.experimental.pallas import tpu as pltpu
from jax.sharding import PartitionSpec as P

CAP = 48
ROWS = 16
LEFT, RIGHT = 0, 1


def row_tile(width):
    for tile in (320, 192, 64, 16):
        if width % tile == 0:
            return tile
    return width


def relay_kernel(
    n_section,
    n_expert,
    tokens_ref,
    gain_ref,
    choice_ref,
    router_ref,
    down_ref,
    up_ref,
    weight_in_ref,
    weight_out_ref,
    out_ref,
    last_sum_ref,
    last_meta_ref,
    x_ref,
    normed,
    arrived,
    gain_col,
    square_sum,
    own_rows,
    gathered,
    partials,
    returned,
    relayed,
    expert_sum,
    expert_own,
    expert_in,
    raw_rows,
    low_own,
    low_in,
    up_previous,
    meta_own,
    meta_in,
    down_v,
    up_v,
    weight_in_v,
    weight_out_v,
    load_sem,
    ag_send,
    ag_recv,
    rs_send,
    rs_recv,
    relay_recv,
    x_send,
    x_recv,
    e_send,
    e_recv,
    m_send,
    m_recv,
    l_send,
    l_recv,
    u_send,
    u_recv,
    out_sem,
):
    section = lax.axis_index("section")
    expert = lax.axis_index("expert")
    hops = choice_ref.shape[0]
    width, rows = x_ref.shape
    tile = row_tile(width)
    steps = n_expert - 1
    following = lax.rem(section + 1, n_section)
    previous = lax.rem(section + n_section - 1, n_section)

    def place(to_section, to_expert):
        return {"section": to_section, "expert": to_expert}

    loads = [
        pltpu.make_async_copy(source, target, load_sem.at[i])
        for i, (source, target) in enumerate(
            (
                (tokens_ref, x_ref),
                (down_ref, down_v),
                (up_ref, up_v),
                (weight_in_ref, weight_in_v),
                (weight_out_ref, weight_out_v),
            )
        )
    ]
    for load in loads:
        load.start()

    barrier = pltpu.get_barrier_semaphore()
    for target in (
        place(following, expert),
        place(previous, expert),
        place(section, lax.rem(expert + 1, n_expert)),
        place(section, lax.rem(expert + n_expert - 1, n_expert)),
        place(section, lax.rem(expert + 2, n_expert)),
    ):
        pl.semaphore_signal(barrier, inc=1, device_id=target, device_id_type=pl.DeviceIdType.MESH)

    pl.semaphore_wait(barrier, 5)

    def remote(source, target, send, recv, device):
        return pltpu.make_async_remote_copy(
            src_ref=source,
            dst_ref=target,
            send_sem=send,
            recv_sem=recv,
            device_id=device,
            device_id_type=pl.DeviceIdType.MESH,
        )

    def tiles(body):
        def step(i, carry):
            body(pl.ds(pl.multiple_of(i * tile, tile), tile))
            return carry

        lax.fori_loop(0, width // tile, step, 0)

    pieces = [(start, min(start + 768, width)) for start in range(0, width, 768)]

    def lane_tiles(start, stop):
        return [(at, min(at + 384, stop)) for at in range(start, stop, 384)]

    def stream_copy(hop, c):
        start, stop = pieces[c]
        return remote(
            x_ref.at[start:stop],
            arrived.at[hop, start:stop],
            x_send.at[hop, c],
            x_recv.at[hop, c],
            place(following, expert),
        )

    loads[0].wait()
    for c in range(len(pieces)):
        stream_copy(0, c).start()

    before = (
        lax.broadcasted_iota(jnp.int32, (rows, rows), 0)
        < lax.broadcasted_iota(jnp.int32, (rows, rows), 1)
    ).astype(jnp.float32).astype(jnp.bfloat16)
    meta_own[...] = jnp.zeros_like(meta_own)
    for hop in range(hops):
        picks = choice_ref[hop]
        mix = router_ref[hop].astype(jnp.float32)
        here = (picks == 0).astype(jnp.float32)
        flag = jnp.max(here, axis=0, keepdims=True)
        position = jnp.dot(
            jnp.broadcast_to(flag, (16, rows)).astype(jnp.bfloat16),
            before,
            preferred_element_type=jnp.float32,
        )[:1]
        chosen = jnp.sum(here * mix, axis=0, keepdims=True)
        total = jnp.sum(mix, axis=0, keepdims=True)
        meta_own[hop, 0:1, :] = jnp.where(flag > 0.0, position, float(CAP))
        meta_own[hop, 1:2, :] = chosen / total

    meta_copy = remote(meta_own, meta_in, m_send, m_recv, place(following, expert))
    meta_copy.start()
    loads[2].wait()
    up_copy = remote(up_v, up_previous, u_send, u_recv, place(following, expert))
    up_copy.start()

    def expert_copy(hop, c):
        at = slice(c * ROWS, (c + 1) * ROWS)
        return remote(
            expert_own.at[hop, at],
            expert_in.at[hop, at],
            e_send.at[hop, c],
            e_recv.at[hop, c],
            place(following, expert),
        )

    def one_hot(meta, hop):
        slots = lax.broadcasted_iota(jnp.int32, (CAP, rows), 0).astype(jnp.float32)
        return jnp.where(slots == meta[hop, 0:1, :], 1.0, 0.0).astype(jnp.bfloat16)

    def select_rows(select, values):
        return lax.dot_general(
            select, values, (((1,), (1,)), ((), ())), preferred_element_type=jnp.float32
        )

    raw_rows[...] = select_rows(one_hot(meta_own, 0), x_ref[...])

    def settle(hop):
        spread = one_hot(meta_in, hop)
        share = meta_in[hop, 1:2, :]
        square_sum[...] = jnp.zeros_like(square_sum)
        for c, (first, last) in enumerate(pieces):
            stream_copy(hop, c).wait_send()
            for start, stop in lane_tiles(first, last):
                picked = lax.dot_general(
                    expert_in[hop, :, start:stop],
                    spread,
                    (((0,), (0,)), ((), ())),
                    preferred_element_type=jnp.float32,
                )
                moved = (
                    arrived[hop, start:stop, :].astype(jnp.float32) + share * picked
                ).astype(jnp.bfloat16)
                x_ref[start:stop, :] = moved
                values = moved.astype(jnp.float32)
                square_sum[...] += jnp.sum(
                    (values * values).reshape((stop - start) // 8, 8, rows), axis=0
                )
            stream_copy(hop + 1, c).start()

    def write_out(c):
        start, stop = pieces[c]
        return pltpu.make_async_copy(
            arrived.at[hops - 1, start:stop], out_ref.at[start:stop], out_sem.at[c]
        )

    def expert_partial(block):
        gate = lax.dot_general(
            block, weight_in_v[0], (((1,), (1,)), ((), ())), preferred_element_type=jnp.float32
        )
        up = lax.dot_general(
            block, weight_in_v[1], (((1,), (1,)), ((), ())), preferred_element_type=jnp.float32
        )
        activated = (gate * jax.nn.sigmoid(1.702 * gate) * (up + 1.0)).astype(jnp.bfloat16)
        return jnp.dot(
            activated, weight_out_v[...], preferred_element_type=jnp.float32
        ).astype(jnp.bfloat16)

    def left_at(distance):
        return expert >= distance

    def right_at(distance):
        return expert + distance < n_expert

    def gather_send(hop, k, side):
        source = own_rows.at[hop] if k == 0 else gathered.at[hop, k - 1, side]
        step = 1 if side == LEFT else -1
        return remote(
            source,
            gathered.at[hop, k, side],
            ag_send.at[hop, k, side],
            ag_recv.at[hop, k, side],
            place(section, lax.rem(expert + step + n_expert, n_expert)),
        )

    def gather_sends(hop, k):
        return (
            (left_at(k) & right_at(1), gather_send(hop, k, LEFT)),
            (right_at(k) & left_at(1), gather_send(hop, k, RIGHT)),
        )

    def piece_of(c):
        return slice(c * ROWS, (c + 1) * ROWS)

    def partial_send(hop, k, side, c):
        away = -(k + 1) if side == LEFT else k + 1
        return remote(
            partials.at[k, side, piece_of(c)],
            returned.at[hop, k, 1 - side, piece_of(c)],
            rs_send.at[hop, k, side, c],
            rs_recv.at[hop, k, 1 - side, c],
            place(section, lax.rem(expert + away + n_expert, n_expert)),
        )

    def relay_send(hop, k, side, c):
        away = -1 if side == LEFT else 1
        return remote(
            partials.at[k, side, piece_of(c)],
            relayed.at[hop, k - 1, side, piece_of(c)],
            rs_send.at[hop, k, side, c],
            relay_recv.at[hop, k - 1, side, c],
            place(section, lax.rem(expert + away + n_expert, n_expert)),
        )

    def at_end(side):
        return expert == (n_expert - 1 if side == LEFT else 0)

    def beside_end(side):
        return expert == (n_expert - 2 if side == LEFT else 1)

    def sends_here(k, side):
        if k == 0:
            return on_side(side, 1)
        return (expert >= k + 2) if side == LEFT else (expert + k + 2 < n_expert)

    def on_side(side, distance):
        return left_at(distance) if side == LEFT else right_at(distance)

    def hop_body(hop, carry):
        raw = raw_rows[...]
        row_scale = lax.rsqrt(
            jnp.sum(raw * raw, axis=1, keepdims=True) * (1.0 / width) + 1e-05
        )
        own_rows[hop] = (raw * row_scale * gain_ref[...]).astype(jnp.bfloat16)
        for valid, copy in gather_sends(hop, 0):
            pl.when(valid)(copy.start)

        @pl.when(hop == 0)
        def _():
            square_sum[...] = jnp.zeros_like(square_sum)

            def first_squares(at):
                values = x_ref[at, :].astype(jnp.float32)
                square_sum[...] += jnp.sum(
                    (values * values).reshape(tile // 8, 8, rows), axis=0
                )

            tiles(first_squares)
            for start in range(0, width, 128):
                stop = min(start + 128, width)
                piece = jnp.broadcast_to(gain_ref[0:1, start:stop], (128, stop - start))
                gain_col[start:stop, :] = piece.T
            loads[1].wait()

        @pl.when(hop > 0)
        def _():
            settle(hop - 1)

        scale = lax.rsqrt(
            jnp.sum(square_sum[...], axis=0, keepdims=True) * (1.0 / width) + 1e-05
        )

        def normalise(at):
            gain = jnp.concatenate([gain_col[at, :]] * (rows // 128), axis=1)
            normed[at, :] = (x_ref[at, :].astype(jnp.float32) * scale * gain).astype(jnp.bfloat16)

        tiles(normalise)
        low_copy = remote(
            low_own.at[hop], low_in.at[hop], l_send.at[hop], l_recv.at[hop], place(following, expert)
        )

        def take_and_forward(k):
            for side in (LEFT, RIGHT):
                pl.when(on_side(side, k + 1))(gather_send(hop, k, side).wait_recv)
            if k + 1 < steps:
                for valid, copy in gather_sends(hop, k + 1):
                    pl.when(valid)(copy.start)

        take_and_forward(0)

        @pl.when(hop == 0)
        def _():
            loads[3].wait()
            loads[4].wait()

        for k in range(steps):

            @pl.when(left_at(k + 1) | right_at(k + 1))
            def _(k=k):
                block = gathered[hop, k].reshape(2 * CAP, width)
                partials[k] = expert_partial(block).reshape(2, CAP, width)

            for side in (LEFT, RIGHT):
                valid = on_side(side, k + 1)
                straight = valid & jnp.logical_not(beside_end(side))
                if k > 0:
                    straight = straight & jnp.logical_not(at_end(side))

                    @pl.when(valid & at_end(side))
                    def _(k=k, side=side):
                        for c in range(CAP // ROWS):
                            relay_send(hop, k, side, c).start()

                @pl.when(straight)
                def _(k=k, side=side):
                    for c in range(CAP // ROWS):
                        partial_send(hop, k, side, c).start()

            if k == 0:
                low_own[hop] = lax.dot_general(
                    down_v[...], normed[...], (((0,), (0,)), ((), ())), preferred_element_type=jnp.float32
                ).astype(jnp.bfloat16)
                low_copy.start()

            if k + 1 < steps:
                take_and_forward(k + 1)

        expert_sum[...] = expert_partial(own_rows[hop]).astype(jnp.float32)

        for k in range(steps - 1):
            for side in (LEFT, RIGHT):

                @pl.when(on_side(side, k + 1) & beside_end(side))
                def _(k=k, side=side):
                    for c in range(CAP // ROWS):
                        relay_send(hop, k + 1, side, c).wait_recv()
                        at = piece_of(c)
                        partials[k, side, at] = (
                            partials[k, side, at].astype(jnp.float32)
                            + relayed[hop, k, side, at].astype(jnp.float32)
                        ).astype(jnp.bfloat16)
                        partial_send(hop, k, side, c).start()

        @pl.when(hop == 0)
        def _():
            meta_copy.wait()
            up_copy.wait()

        low_copy.wait()
        more = hop + 1 < hops

        def adapt(c):
            first, last = pieces[c]
            stream_copy(hop, c).wait_recv()
            for start, stop in lane_tiles(first, last):
                arrived[hop, start:stop, :] = (
                    arrived[hop, start:stop, :].astype(jnp.float32)
                    + jnp.dot(
                        up_previous[start:stop, :], low_in[hop], preferred_element_type=jnp.float32
                    )
                ).astype(jnp.bfloat16)

            @pl.when(more)
            def _():
                raw_rows[:, first:last] = select_rows(
                    one_hot(meta_own, hop + 1), arrived[hop, first:last, :]
                )

            @pl.when(hop + 1 == hops)
            def _():
                write_out(c).start()

        for c in range(len(pieces) - 1):
            adapt(c)

        for c in range(CAP // ROWS):
            at = piece_of(c)
            for k in range(steps):
                for side in (LEFT, RIGHT):

                    @pl.when(sends_here(k, side))
                    def _(k=k, side=side, c=c, at=at):
                        partial_send(hop, k, 1 - side, c).wait_recv()
                        expert_sum[at] += returned[hop, k, side, at].astype(jnp.float32)

            expert_own[hop, at] = expert_sum[at].astype(jnp.bfloat16)
            expert_copy(hop, c).start()

        adapt(len(pieces) - 1)

        for k in range(steps):
            for valid, copy in gather_sends(hop, k):
                pl.when(valid)(copy.wait_send)
            for side in (LEFT, RIGHT):
                for c in range(CAP // ROWS):
                    pl.when(on_side(side, k + 1))(partial_send(hop, k, side, c).wait_send)

        @pl.when(more)
        def _():
            chosen = one_hot(meta_own, hop + 1)
            meeting = select_rows(chosen, one_hot(meta_in, hop)).astype(jnp.bfloat16)
            share = jnp.sum(
                chosen.astype(jnp.float32) * meta_in[hop, 1:2, :], axis=1, keepdims=True
            )
            for c in range(CAP // ROWS):
                expert_copy(hop, c).wait()
            picked = jnp.dot(meeting, expert_in[hop], preferred_element_type=jnp.float32)
            raw_rows[...] = (
                (raw_rows[...] + share * picked).astype(jnp.bfloat16).astype(jnp.float32)
            )

        @pl.when(hop + 1 == hops)
        def _():
            for c in range(CAP // ROWS):
                expert_copy(hop, c).wait()

        return carry

    lax.fori_loop(0, hops, hop_body, 0)
    last_sum_ref[...] = expert_in[hops - 1]
    last_meta_ref[...] = meta_in[hops - 1]
    for c in range(len(pieces)):
        stream_copy(hops - 1, c).wait_send()
        write_out(c).wait()


def last_kernel(adapted_ref, expert_ref, meta_ref, out_ref):
    rows = out_ref.shape[1]
    slots = lax.broadcasted_iota(jnp.int32, (CAP, rows), 0).astype(jnp.float32)
    spread = jnp.where(slots == meta_ref[0:1, :], 1.0, 0.0).astype(jnp.bfloat16)
    picked = lax.dot_general(
        expert_ref[...], spread, (((0,), (0,)), ((), ())), preferred_element_type=jnp.float32
    )
    out_ref[...] = (
        adapted_ref[...].astype(jnp.float32) + meta_ref[1:2, :] * picked
    ).astype(out_ref.dtype)


def body(
    n_section,
    n_expert,
    tokens,
    segment_norm_scale,
    expert_choice_table,
    router_weight_table,
    adapter_down_weight,
    adapter_up_weight,
    expert_gate_up_weight,
    expert_down_weight,
):
    rows, width = tokens.shape
    hops, _, top = expert_choice_table.shape
    rank = adapter_down_weight.shape[2]
    hid = expert_down_weight.shape[1]
    steps = n_expert - 1
    stream_pieces = pl.cdiv(width, 768)
    half = jnp.bfloat16
    full = jnp.float32
    block = (CAP, width)
    dma = pltpu.SemaphoreType.DMA
    flops = hops * (4 * rows * width * rank + 6 * n_expert * CAP * width * hid)
    adapted, last_sum, last_meta = pl.pallas_call(
        functools.partial(relay_kernel, n_section, n_expert),
        out_shape=(
            jax.ShapeDtypeStruct((width, rows), half),
            jax.ShapeDtypeStruct(block, half),
            jax.ShapeDtypeStruct((8, rows), full),
        ),
        in_specs=[
            pl.BlockSpec(memory_space=pl.ANY),
            pl.BlockSpec(memory_space=pltpu.VMEM),
            pl.BlockSpec(memory_space=pltpu.VMEM),
            pl.BlockSpec(memory_space=pltpu.VMEM),
            pl.BlockSpec(memory_space=pl.ANY),
            pl.BlockSpec(memory_space=pl.ANY),
            pl.BlockSpec(memory_space=pl.ANY),
            pl.BlockSpec(memory_space=pl.ANY),
        ],
        out_specs=(
            pl.BlockSpec(memory_space=pl.ANY),
            pl.BlockSpec(memory_space=pltpu.VMEM),
            pl.BlockSpec(memory_space=pltpu.VMEM),
        ),
        scratch_shapes=[
            pltpu.VMEM((width, rows), half),
            pltpu.VMEM((width, rows), half),
            pltpu.VMEM((hops, width, rows), half),
            pltpu.VMEM((width, 128), full),
            pltpu.VMEM((8, rows), full),
            pltpu.VMEM((hops,) + block, half),
            pltpu.VMEM((hops, steps, 2) + block, half),
            pltpu.VMEM((steps, 2) + block, half),
            pltpu.VMEM((hops, steps, 2) + block, half),
            pltpu.VMEM((hops, steps - 1, 2) + block, half),
            pltpu.VMEM(block, full),
            pltpu.VMEM((hops,) + block, half),
            pltpu.VMEM((hops,) + block, half),
            pltpu.VMEM(block, full),
            pltpu.VMEM((hops, rank, rows), half),
            pltpu.VMEM((hops, rank, rows), half),
            pltpu.VMEM((width, rank), half),
            pltpu.VMEM((hops, 8, rows), full),
            pltpu.VMEM((hops, 8, rows), full),
            pltpu.VMEM((width, rank), half),
            pltpu.VMEM((width, rank), half),
            pltpu.VMEM((2, hid, width), half),
            pltpu.VMEM((hid, width), half),
            dma((5,)),
            dma((hops, steps, 2)),
            dma((hops, steps, 2)),
            dma((hops, steps, 2, CAP // ROWS)),
            dma((hops, steps, 2, CAP // ROWS)),
            dma((hops, steps - 1, 2, CAP // ROWS)),
            dma((hops, stream_pieces)),
            dma((hops, stream_pieces)),
            dma((hops, CAP // ROWS)),
            dma((hops, CAP // ROWS)),
            dma,
            dma,
            dma((hops,)),
            dma((hops,)),
            dma,
            dma,
            dma((stream_pieces,)),
        ],
        compiler_params=pltpu.CompilerParams(
            collective_id=0, has_side_effects=True, vmem_limit_bytes=60 * 2**20
        ),
        cost_estimate=pl.CostEstimate(
            flops=flops, bytes_accessed=16 * 2**20, transcendentals=hops * n_expert * CAP * hid
        ),
    )(
        tokens.T,
        segment_norm_scale,
        jnp.transpose(expert_choice_table, (0, 2, 1)),
        jnp.transpose(router_weight_table, (0, 2, 1)),
        adapter_down_weight[0],
        adapter_up_weight[0].T,
        jnp.transpose(expert_gate_up_weight[0], (1, 2, 0)),
        expert_down_weight[0],
    )
    lanes = 768
    out = pl.pallas_call(
        last_kernel,
        out_shape=jax.ShapeDtypeStruct((width, rows), half),
        grid=(pl.cdiv(width, lanes),),
        in_specs=[
            pl.BlockSpec((lanes, rows), lambda i: (i, 0)),
            pl.BlockSpec((CAP, lanes), lambda i: (0, i)),
            pl.BlockSpec((8, rows), lambda i: (0, 0)),
        ],
        out_specs=pl.BlockSpec((lanes, rows), lambda i: (i, 0)),
        cost_estimate=pl.CostEstimate(
            flops=2 * CAP * width * rows, bytes_accessed=4 * width * rows, transcendentals=0
        ),
    )(adapted, last_sum, last_meta)
    return out.T


def solution(mesh):
    return jax.shard_map(
        functools.partial(body, mesh.shape["section"], mesh.shape["expert"]),
        mesh=mesh,
        in_specs=(
            P(("section", "expert"), None),
            P("section", None),
            P(None, ("section", "expert"), None),
            P(None, ("section", "expert"), None),
            P("section", None, None),
            P("section", None, None),
            P("section", None, None, "expert"),
            P("section", "expert", None),
        ),
        out_specs=P(("section", "expert"), None),
        check_vma=False,
    )
```

```python
import functools

import jax
import jax.numpy as jnp
from jax import lax
from jax.experimental import pallas as pl
from jax.experimental.pallas import tpu as pltpu
from jax.sharding import PartitionSpec as P

CAP = 48
ROWS = 16
RAW_PIECES = 2
LEFT, RIGHT = 0, 1


def row_tile(width):
    for tile in (320, 192, 64, 16):
        if width % tile == 0:
            return tile
    return width


def relay_kernel(
    n_section,
    n_expert,
    tokens_ref,
    gain_ref,
    choice_ref,
    router_ref,
    down_ref,
    up_ref,
    weight_in_ref,
    weight_out_ref,
    out_ref,
    last_sum_ref,
    last_meta_ref,
    x_ref,
    normed,
    arrived,
    gain_col,
    square_sum,
    own_rows,
    gathered,
    partials,
    returned,
    relayed,
    expert_sum,
    expert_own,
    expert_in,
    raw_rows,
    low_own,
    low_in,
    up_previous,
    meta_own,
    meta_in,
    down_v,
    up_v,
    weight_in_v,
    weight_out_v,
    load_sem,
    ag_send,
    ag_recv,
    rs_send,
    rs_recv,
    relay_recv,
    x_send,
    x_recv,
    e_send,
    e_recv,
    m_send,
    m_recv,
    l_send,
    l_recv,
    u_send,
    u_recv,
    out_sem,
):
    section = lax.axis_index("section")
    expert = lax.axis_index("expert")
    hops = choice_ref.shape[0]
    width, rows = x_ref.shape
    tile = row_tile(width)
    steps = n_expert - 1
    following = lax.rem(section + 1, n_section)
    previous = lax.rem(section + n_section - 1, n_section)

    def place(to_section, to_expert):
        return {"section": to_section, "expert": to_expert}

    loads = [
        pltpu.make_async_copy(source, target, load_sem.at[i])
        for i, (source, target) in enumerate(
            (
                (tokens_ref, x_ref),
                (down_ref, down_v),
                (up_ref, up_v),
                (weight_in_ref, weight_in_v),
                (weight_out_ref, weight_out_v),
            )
        )
    ]
    for load in loads:
        load.start()

    barrier = pltpu.get_barrier_semaphore()
    for target in (
        place(following, expert),
        place(previous, expert),
        place(section, lax.rem(expert + 1, n_expert)),
        place(section, lax.rem(expert + n_expert - 1, n_expert)),
        place(section, lax.rem(expert + 2, n_expert)),
    ):
        pl.semaphore_signal(barrier, inc=1, device_id=target, device_id_type=pl.DeviceIdType.MESH)

    pl.semaphore_wait(barrier, 5)

    def remote(source, target, send, recv, device):
        return pltpu.make_async_remote_copy(
            src_ref=source,
            dst_ref=target,
            send_sem=send,
            recv_sem=recv,
            device_id=device,
            device_id_type=pl.DeviceIdType.MESH,
        )

    def tiles(body):
        def step(i, carry):
            body(pl.ds(pl.multiple_of(i * tile, tile), tile))
            return carry

        lax.fori_loop(0, width // tile, step, 0)

    pieces = [(start, min(start + 768, width)) for start in range(0, width, 768)]

    def lane_tiles(start, stop):
        return [(at, min(at + 384, stop)) for at in range(start, stop, 384)]

    def stream_copy(hop, c):
        start, stop = pieces[c]
        return remote(
            x_ref.at[start:stop],
            arrived.at[hop, start:stop],
            x_send.at[hop, c],
            x_recv.at[hop, c],
            place(following, expert),
        )

    loads[0].wait()
    for c in range(RAW_PIECES):
        stream_copy(0, c).start()

    before = (
        lax.broadcasted_iota(jnp.int32, (rows, rows), 0)
        < lax.broadcasted_iota(jnp.int32, (rows, rows), 1)
    ).astype(jnp.float32).astype(jnp.bfloat16)
    meta_own[...] = jnp.zeros_like(meta_own)
    for hop in range(hops):
        picks = choice_ref[hop]
        mix = router_ref[hop].astype(jnp.float32)
        here = (picks == 0).astype(jnp.float32)
        flag = jnp.max(here, axis=0, keepdims=True)
        position = jnp.dot(
            jnp.broadcast_to(flag, (16, rows)).astype(jnp.bfloat16),
            before,
            preferred_element_type=jnp.float32,
        )[:1]
        chosen = jnp.sum(here * mix, axis=0, keepdims=True)
        total = jnp.sum(mix, axis=0, keepdims=True)
        meta_own[hop, 0:1, :] = jnp.where(flag > 0.0, position, float(CAP))
        meta_own[hop, 1:2, :] = chosen / total

    meta_copy = remote(meta_own, meta_in, m_send, m_recv, place(following, expert))
    meta_copy.start()
    loads[2].wait()
    first_rows = pieces[RAW_PIECES - 1][1]
    up_copy = remote(
        up_v.at[0:first_rows], up_previous, u_send, u_recv, place(following, expert))
    up_copy.start()

    def expert_copy(hop, c):
        at = slice(c * ROWS, (c + 1) * ROWS)
        return remote(
            expert_own.at[hop, at],
            expert_in.at[hop, at],
            e_send.at[hop, c],
            e_recv.at[hop, c],
            place(following, expert),
        )

    def add_adapter(rows_ref, up_rows, low):
        rows_ref[...] = (
            rows_ref[...].astype(jnp.float32)
            + jnp.dot(up_rows, low, preferred_element_type=jnp.float32)
        ).astype(jnp.bfloat16)

    def one_hot(meta, hop):
        slots = lax.broadcasted_iota(jnp.int32, (CAP, rows), 0).astype(jnp.float32)
        return jnp.where(slots == meta[hop, 0:1, :], 1.0, 0.0).astype(jnp.bfloat16)

    def select_rows(select, values):
        return lax.dot_general(
            select, values, (((1,), (1,)), ((), ())), preferred_element_type=jnp.float32
        )

    raw_rows[...] = select_rows(one_hot(meta_own, 0), x_ref[...])

    def settle(hop):
        spread = one_hot(meta_in, hop)
        share = meta_in[hop, 1:2, :]
        square_sum[...] = jnp.zeros_like(square_sum)
        for c, (first, last) in enumerate(pieces):
            stream_copy(hop, c).wait_send()
            for start, stop in lane_tiles(first, last):
                picked = lax.dot_general(
                    expert_in[hop, :, start:stop],
                    spread,
                    (((0,), (0,)), ((), ())),
                    preferred_element_type=jnp.float32,
                )
                moved = (
                    arrived[hop, start:stop, :].astype(jnp.float32) + share * picked
                ).astype(jnp.bfloat16)
                x_ref[start:stop, :] = moved
                values = moved.astype(jnp.float32)
                square_sum[...] += jnp.sum(
                    (values * values).reshape((stop - start) // 8, 8, rows), axis=0
                )
            if c < RAW_PIECES:
                stream_copy(hop + 1, c).start()

    def write_out(c):
        start, stop = pieces[c]
        return pltpu.make_async_copy(
            arrived.at[hops - 1, start:stop], out_ref.at[start:stop], out_sem.at[c]
        )

    def expert_partial(block):
        gate = lax.dot_general(
            block, weight_in_v[0], (((1,), (1,)), ((), ())), preferred_element_type=jnp.float32
        )
        up = lax.dot_general(
            block, weight_in_v[1], (((1,), (1,)), ((), ())), preferred_element_type=jnp.float32
        )
        activated = (gate * jax.nn.sigmoid(1.702 * gate) * (up + 1.0)).astype(jnp.bfloat16)
        return jnp.dot(
            activated, weight_out_v[...], preferred_element_type=jnp.float32
        ).astype(jnp.bfloat16)

    def left_at(distance):
        return expert >= distance

    def right_at(distance):
        return expert + distance < n_expert

    def gather_send(hop, k, side):
        source = own_rows.at[hop] if k == 0 else gathered.at[hop, k - 1, side]
        step = 1 if side == LEFT else -1
        return remote(
            source,
            gathered.at[hop, k, side],
            ag_send.at[hop, k, side],
            ag_recv.at[hop, k, side],
            place(section, lax.rem(expert + step + n_expert, n_expert)),
        )

    def gather_sends(hop, k):
        return (
            (left_at(k) & right_at(1), gather_send(hop, k, LEFT)),
            (right_at(k) & left_at(1), gather_send(hop, k, RIGHT)),
        )

    def piece_of(c):
        return slice(c * ROWS, (c + 1) * ROWS)

    def partial_send(hop, k, side, c):
        away = -(k + 1) if side == LEFT else k + 1
        return remote(
            partials.at[k, side, piece_of(c)],
            returned.at[hop, k, 1 - side, piece_of(c)],
            rs_send.at[hop, k, side, c],
            rs_recv.at[hop, k, 1 - side, c],
            place(section, lax.rem(expert + away + n_expert, n_expert)),
        )

    def relay_send(hop, k, side, c):
        away = -1 if side == LEFT else 1
        return remote(
            partials.at[k, side, piece_of(c)],
            relayed.at[hop, k - 1, side, piece_of(c)],
            rs_send.at[hop, k, side, c],
            relay_recv.at[hop, k - 1, side, c],
            place(section, lax.rem(expert + away + n_expert, n_expert)),
        )

    def at_end(side):
        return expert == (n_expert - 1 if side == LEFT else 0)

    def beside_end(side):
        return expert == (n_expert - 2 if side == LEFT else 1)

    def sends_here(k, side):
        if k == 0:
            return on_side(side, 1)
        return (expert >= k + 2) if side == LEFT else (expert + k + 2 < n_expert)

    def on_side(side, distance):
        return left_at(distance) if side == LEFT else right_at(distance)

    def hop_body(hop, carry):
        raw = raw_rows[...]
        row_scale = lax.rsqrt(
            jnp.sum(raw * raw, axis=1, keepdims=True) * (1.0 / width) + 1e-05
        )
        own_rows[hop] = (raw * row_scale * gain_ref[...]).astype(jnp.bfloat16)
        for valid, copy in gather_sends(hop, 0):
            pl.when(valid)(copy.start)

        @pl.when(hop == 0)
        def _():
            square_sum[...] = jnp.zeros_like(square_sum)

            def first_squares(at):
                values = x_ref[at, :].astype(jnp.float32)
                square_sum[...] += jnp.sum(
                    (values * values).reshape(tile // 8, 8, rows), axis=0
                )

            tiles(first_squares)
            for start in range(0, width, 128):
                stop = min(start + 128, width)
                piece = jnp.broadcast_to(gain_ref[0:1, start:stop], (128, stop - start))
                gain_col[start:stop, :] = piece.T
            loads[1].wait()

        @pl.when(hop > 0)
        def _():
            settle(hop - 1)

        scale = lax.rsqrt(
            jnp.sum(square_sum[...], axis=0, keepdims=True) * (1.0 / width) + 1e-05
        )

        def normalise(at):
            gain = jnp.concatenate([gain_col[at, :]] * (rows // 128), axis=1)
            normed[at, :] = (x_ref[at, :].astype(jnp.float32) * scale * gain).astype(jnp.bfloat16)

        tiles(normalise)
        low_copy = remote(
            low_own.at[hop], low_in.at[hop], l_send.at[hop], l_recv.at[hop], place(following, expert)
        )

        def take_and_forward(k):
            for side in (LEFT, RIGHT):
                pl.when(on_side(side, k + 1))(gather_send(hop, k, side).wait_recv)
            if k + 1 < steps:
                for valid, copy in gather_sends(hop, k + 1):
                    pl.when(valid)(copy.start)

        take_and_forward(0)

        @pl.when(hop == 0)
        def _():
            loads[3].wait()
            loads[4].wait()

        for k in range(steps):

            @pl.when(left_at(k + 1) | right_at(k + 1))
            def _(k=k):
                block = gathered[hop, k].reshape(2 * CAP, width)
                partials[k] = expert_partial(block).reshape(2, CAP, width)

            for side in (LEFT, RIGHT):
                valid = on_side(side, k + 1)
                straight = valid & jnp.logical_not(beside_end(side))
                if k > 0:
                    straight = straight & jnp.logical_not(at_end(side))

                    @pl.when(valid & at_end(side))
                    def _(k=k, side=side):
                        for c in range(CAP // ROWS):
                            relay_send(hop, k, side, c).start()

                @pl.when(straight)
                def _(k=k, side=side):
                    for c in range(CAP // ROWS):
                        partial_send(hop, k, side, c).start()

            if k == 0:
                low_own[hop] = lax.dot_general(
                    down_v[...], normed[...], (((0,), (0,)), ((), ())), preferred_element_type=jnp.float32
                ).astype(jnp.bfloat16)
                low_copy.start()

            if k + 1 < steps:
                take_and_forward(k + 1)
            if k == 0:
                for c in range(RAW_PIECES, len(pieces)):
                    for start, stop in lane_tiles(*pieces[c]):
                        add_adapter(x_ref.at[start:stop], up_v[start:stop, :], low_own[hop])
                    stream_copy(hop, c).start()

        expert_sum[...] = expert_partial(own_rows[hop]).astype(jnp.float32)

        for k in range(steps - 1):
            for side in (LEFT, RIGHT):

                @pl.when(on_side(side, k + 1) & beside_end(side))
                def _(k=k, side=side):
                    for c in range(CAP // ROWS):
                        relay_send(hop, k + 1, side, c).wait_recv()
                        at = piece_of(c)
                        partials[k, side, at] = (
                            partials[k, side, at].astype(jnp.float32)
                            + relayed[hop, k, side, at].astype(jnp.float32)
                        ).astype(jnp.bfloat16)
                        partial_send(hop, k, side, c).start()

        @pl.when(hop == 0)
        def _():
            meta_copy.wait()
            up_copy.wait()

        low_copy.wait()
        more = hop + 1 < hops

        def adapt(c):
            first, last = pieces[c]
            stream_copy(hop, c).wait_recv()
            if c < RAW_PIECES:
                for start, stop in lane_tiles(first, last):
                    add_adapter(
                        arrived.at[hop, start:stop], up_previous[start:stop, :], low_in[hop]
                    )

            @pl.when(more)
            def _():
                raw_rows[:, first:last] = select_rows(
                    one_hot(meta_own, hop + 1), arrived[hop, first:last, :]
                )

            @pl.when(hop + 1 == hops)
            def _():
                write_out(c).start()

        for c in range(len(pieces) - 1):
            adapt(c)

        for c in range(CAP // ROWS):
            at = piece_of(c)
            for k in range(steps):
                for side in (LEFT, RIGHT):

                    @pl.when(sends_here(k, side))
                    def _(k=k, side=side, c=c, at=at):
                        partial_send(hop, k, 1 - side, c).wait_recv()
                        expert_sum[at] += returned[hop, k, side, at].astype(jnp.float32)

            expert_own[hop, at] = expert_sum[at].astype(jnp.bfloat16)
            expert_copy(hop, c).start()

        adapt(len(pieces) - 1)

        for k in range(steps):
            for valid, copy in gather_sends(hop, k):
                pl.when(valid)(copy.wait_send)
            for side in (LEFT, RIGHT):
                for c in range(CAP // ROWS):
                    pl.when(on_side(side, k + 1))(partial_send(hop, k, side, c).wait_send)

        @pl.when(more)
        def _():
            chosen = one_hot(meta_own, hop + 1)
            meeting = select_rows(chosen, one_hot(meta_in, hop)).astype(jnp.bfloat16)
            share = jnp.sum(
                chosen.astype(jnp.float32) * meta_in[hop, 1:2, :], axis=1, keepdims=True
            )
            for c in range(CAP // ROWS):
                expert_copy(hop, c).wait()
            picked = jnp.dot(meeting, expert_in[hop], preferred_element_type=jnp.float32)
            raw_rows[...] = (
                (raw_rows[...] + share * picked).astype(jnp.bfloat16).astype(jnp.float32)
            )

        @pl.when(hop + 1 == hops)
        def _():
            for c in range(CAP // ROWS):
                expert_copy(hop, c).wait()

        return carry

    lax.fori_loop(0, hops, hop_body, 0)
    last_sum_ref[...] = expert_in[hops - 1]
    last_meta_ref[...] = meta_in[hops - 1]
    for c in range(len(pieces)):
        stream_copy(hops - 1, c).wait_send()
        write_out(c).wait()


def last_kernel(adapted_ref, expert_ref, meta_ref, out_ref):
    rows = out_ref.shape[1]
    slots = lax.broadcasted_iota(jnp.int32, (CAP, rows), 0).astype(jnp.float32)
    spread = jnp.where(slots == meta_ref[0:1, :], 1.0, 0.0).astype(jnp.bfloat16)
    picked = lax.dot_general(
        expert_ref[...], spread, (((0,), (0,)), ((), ())), preferred_element_type=jnp.float32
    )
    out_ref[...] = (
        adapted_ref[...].astype(jnp.float32) + meta_ref[1:2, :] * picked
    ).astype(out_ref.dtype)


def body(
    n_section,
    n_expert,
    tokens,
    segment_norm_scale,
    expert_choice_table,
    router_weight_table,
    adapter_down_weight,
    adapter_up_weight,
    expert_gate_up_weight,
    expert_down_weight,
):
    rows, width = tokens.shape
    hops, _, top = expert_choice_table.shape
    rank = adapter_down_weight.shape[2]
    hid = expert_down_weight.shape[1]
    steps = n_expert - 1
    stream_pieces = pl.cdiv(width, 768)
    half = jnp.bfloat16
    full = jnp.float32
    block = (CAP, width)
    dma = pltpu.SemaphoreType.DMA
    flops = hops * (4 * rows * width * rank + 6 * n_expert * CAP * width * hid)
    adapted, last_sum, last_meta = pl.pallas_call(
        functools.partial(relay_kernel, n_section, n_expert),
        out_shape=(
            jax.ShapeDtypeStruct((width, rows), half),
            jax.ShapeDtypeStruct(block, half),
            jax.ShapeDtypeStruct((8, rows), full),
        ),
        in_specs=[
            pl.BlockSpec(memory_space=pl.ANY),
            pl.BlockSpec(memory_space=pltpu.VMEM),
            pl.BlockSpec(memory_space=pltpu.VMEM),
            pl.BlockSpec(memory_space=pltpu.VMEM),
            pl.BlockSpec(memory_space=pl.ANY),
            pl.BlockSpec(memory_space=pl.ANY),
            pl.BlockSpec(memory_space=pl.ANY),
            pl.BlockSpec(memory_space=pl.ANY),
        ],
        out_specs=(
            pl.BlockSpec(memory_space=pl.ANY),
            pl.BlockSpec(memory_space=pltpu.VMEM),
            pl.BlockSpec(memory_space=pltpu.VMEM),
        ),
        scratch_shapes=[
            pltpu.VMEM((width, rows), half),
            pltpu.VMEM((width, rows), half),
            pltpu.VMEM((hops, width, rows), half),
            pltpu.VMEM((width, 128), full),
            pltpu.VMEM((8, rows), full),
            pltpu.VMEM((hops,) + block, half),
            pltpu.VMEM((hops, steps, 2) + block, half),
            pltpu.VMEM((steps, 2) + block, half),
            pltpu.VMEM((hops, steps, 2) + block, half),
            pltpu.VMEM((hops, steps - 1, 2) + block, half),
            pltpu.VMEM(block, full),
            pltpu.VMEM((hops,) + block, half),
            pltpu.VMEM((hops,) + block, half),
            pltpu.VMEM(block, full),
            pltpu.VMEM((hops, rank, rows), half),
            pltpu.VMEM((hops, rank, rows), half),
            pltpu.VMEM((min(width, 768 * RAW_PIECES), rank), half),
            pltpu.VMEM((hops, 8, rows), full),
            pltpu.VMEM((hops, 8, rows), full),
            pltpu.VMEM((width, rank), half),
            pltpu.VMEM((width, rank), half),
            pltpu.VMEM((2, hid, width), half),
            pltpu.VMEM((hid, width), half),
            dma((5,)),
            dma((hops, steps, 2)),
            dma((hops, steps, 2)),
            dma((hops, steps, 2, CAP // ROWS)),
            dma((hops, steps, 2, CAP // ROWS)),
            dma((hops, steps - 1, 2, CAP // ROWS)),
            dma((hops, stream_pieces)),
            dma((hops, stream_pieces)),
            dma((hops, CAP // ROWS)),
            dma((hops, CAP // ROWS)),
            dma,
            dma,
            dma((hops,)),
            dma((hops,)),
            dma,
            dma,
            dma((stream_pieces,)),
        ],
        compiler_params=pltpu.CompilerParams(
            collective_id=0, has_side_effects=True, vmem_limit_bytes=60 * 2**20
        ),
        cost_estimate=pl.CostEstimate(
            flops=flops, bytes_accessed=16 * 2**20, transcendentals=hops * n_expert * CAP * hid
        ),
    )(
        tokens.T,
        segment_norm_scale,
        jnp.transpose(expert_choice_table, (0, 2, 1)),
        jnp.transpose(router_weight_table, (0, 2, 1)),
        adapter_down_weight[0],
        adapter_up_weight[0].T,
        jnp.transpose(expert_gate_up_weight[0], (1, 2, 0)),
        expert_down_weight[0],
    )
    lanes = 768
    out = pl.pallas_call(
        last_kernel,
        out_shape=jax.ShapeDtypeStruct((width, rows), half),
        grid=(pl.cdiv(width, lanes),),
        in_specs=[
            pl.BlockSpec((lanes, rows), lambda i: (i, 0)),
            pl.BlockSpec((CAP, lanes), lambda i: (0, i)),
            pl.BlockSpec((8, rows), lambda i: (0, 0)),
        ],
        out_specs=pl.BlockSpec((lanes, rows), lambda i: (i, 0)),
        cost_estimate=pl.CostEstimate(
            flops=2 * CAP * width * rows, bytes_accessed=4 * width * rows, transcendentals=0
        ),
    )(adapted, last_sum, last_meta)
    return out.T


def solution(mesh):
    return jax.shard_map(
        functools.partial(body, mesh.shape["section"], mesh.shape["expert"]),
        mesh=mesh,
        in_specs=(
            P(("section", "expert"), None),
            P("section", None),
            P(None, ("section", "expert"), None),
            P(None, ("section", "expert"), None),
            P("section", None, None),
            P("section", None, None),
            P("section", None, None, "expert"),
            P("section", "expert", None),
        ),
        out_specs=P(("section", "expert"), None),
        check_vma=False,
    )
```
